32 devices in a mesh: plane: 16 (over z, x, core), mode: 2 (over y).
Axes of the slice: x: 2, y: 2, z: 4, core: 2. Of those that a mesh axis runs over, the one named last changes fastest.
Arguments:
- velocity: float32 [3, 12800, 1024], P(None, 'plane', 'mode'), may hold values from -10 to 10
- inverses: float32 [512, 25, 25], P('mode'), may hold values from -1 to 2
- neighbours: int32 [512, 4], P('plane'), may hold values from -1 to 31, as said below
- flags: int32 [512], P('plane'), may hold values 0 or 1
Outputs:
- advanced: float32 [3, 12800, 1024], P(None, 'plane', 'mode')
- viscosity: float32 [512], P('plane')
The draws below stay inside these ranges and needn't reach their ends.
Inputs may be any that keep to these rules, and one draw needn't show every extreme that they name: Partition q holds one column of 32 elements of a structured patch, numbered in its own order; every element of it has its west neighbour in partition q - 1 and its east neighbour in partition q + 1 (none in the first and last partitions), its south and north neighbours in q, with -1 only at the patch's edges.
All inputs are finite; a program needn't handle non-finite values. No bound on the sum of `flags` on one device may be relied on, other than what follows from the above.
Results may differ from the reference program's by a relative error of at most 0.000062.
Values sent between devices are 32-bit elements; how exact they have to be, the bound alone decides.
No kernel may reach another device: no remote copies, remote signals or barrier semaphores. Data moves between devices by JAX's collectives and lax.ppermute only.
A program may use at most 128 MiB of HBM per device.

```python
import math
import jax
import jax.numpy as jnp
from jax import lax

ORDER = 4
NODES = 25
MODES = 512
COEFS = 1024
E_DEV = 32
ELEMS = 512
NPTS = 12800
N_PLANE = 16


def draw_velocity(key, part):
    key_base, key_high = jax.random.split(key, 2)
    element = jnp.arange(ELEMS)
    column = (element // E_DEV).astype(jnp.float32) / max(N_PLANE - 1, 1)
    high_share = jnp.exp(jax.random.uniform(key_high, (ELEMS,), jnp.float32, math.log(0.03), 0.0))
    node = jnp.arange(NODES)
    is_high = (node // (ORDER + 1) == ORDER) | (node % (ORDER + 1) == ORDER)
    pair = (jnp.arange(COEFS) // 2).astype(jnp.float32)
    mode_scale = jnp.exp(-math.log(3.0) * pair / (2.0 * MODES))
    base = jnp.clip(jax.random.normal(key_base, (3, ELEMS, NODES, COEFS), jnp.float32), -4.0, 4.0)
    trend = jnp.exp(math.log(3.0) * (0.5 * column - 0.25))
    element_scale = trend
    node_scale = jnp.where(is_high[None, :], high_share[:, None], 1.0)
    full = base * (element_scale[:, None] * node_scale)[None, :, :, None] * mode_scale
    return full.reshape(3, ELEMS * NODES, COEFS)


def draw_inverses(key, part):
    key_diag, key_off = jax.random.split(key, 2)
    mode = jnp.arange(MODES).astype(jnp.float32)
    damp = 1.0 / (1.0 + mode / MODES)
    identity = jnp.eye(NODES, dtype=jnp.float32)
    diagonal = jax.random.uniform(key_diag, (MODES, NODES), jnp.float32, 1.0, 1.5)
    off_diag = jnp.clip(0.06 * jax.random.normal(key_off, (MODES, NODES, NODES), jnp.float32), -0.3, 0.3)
    matrix = identity * diagonal[:, :, None] + off_diag * (1.0 - identity)
    return matrix * damp[:, None, None]


def draw_neighbours(key, part):
    keys = jax.random.split(key, N_PLANE)
    perms = jax.vmap(lambda single: jax.random.permutation(single, E_DEV))(keys).astype(jnp.int32)
    rows = jnp.argsort(perms, axis=1).astype(jnp.int32)
    column = jnp.arange(N_PLANE, dtype=jnp.int32)[:, None]
    west = jnp.where(column > 0, perms[jnp.maximum(column - 1, 0), rows], -1)
    east = jnp.where(column < N_PLANE - 1, perms[jnp.minimum(column + 1, N_PLANE - 1), rows], -1)
    south = jnp.where(rows > 0, perms[column, jnp.maximum(rows - 1, 0)], -1)
    north = jnp.where(rows < E_DEV - 1, perms[column, jnp.minimum(rows + 1, E_DEV - 1)], -1)
    listed = jnp.stack([west, east, south, north], axis=2)
    return listed.reshape(ELEMS, 4).astype(jnp.int32)


def set_ends(drawn, own_key, low, largest):
    extent = drawn.shape
    index_at = [jax.random.randint(jax.random.fold_in(own_key, axis), (), 0, extent[axis]) for axis in range(len(extent))]
    drawn = drawn.at[tuple(index_at)].set(low)
    longest = extent.index(max(extent))
    index_at[longest] = (index_at[longest] + 1) % extent[longest]
    return drawn.at[tuple(index_at)].set(largest)


def setup_inputs(seed: int = 0) -> dict:
    key_list = jax.random.split(jax.random.key(seed), 5)
    velocity = draw_velocity(jax.random.fold_in(key_list[4], 71), 0)
    inverses = draw_inverses(jax.random.fold_in(key_list[4], 71), 0)
    neighbours = draw_neighbours(jax.random.fold_in(key_list[4], 71), 0)
    flags = set_ends((jax.random.randint(key_list[3], (ELEMS,), 0, 2) < 1).astype(jnp.int32), jax.random.fold_in(key_list[3], 1), 0, 1)
    return dict(velocity=velocity, inverses=inverses, neighbours=neighbours, flags=flags)


highest = lax.Precision.HIGHEST

def basis_table():
    index = jnp.arange(COEFS, dtype=jnp.int32)
    pair = index // 2
    slot = index % 2
    freq = jnp.where((slot == 1) & (pair == 0), MODES, pair)
    phase = freq[:, None] * index[None, :] % COEFS
    angle = phase.astype(jnp.float32) * (2.0 * math.pi / COEFS)
    use_cos = (slot == 0) | (pair == 0)
    basis = jnp.where(use_cos[:, None], jnp.cos(angle), -jnp.sin(angle))
    weight = jnp.where(pair == 0, 1.0, 2.0).astype(jnp.float32)
    return (basis, weight)

def spanwise_term(flux_modes):
    index = jnp.arange(COEFS, dtype=jnp.int32)
    pair = index // 2
    rate = pair.astype(jnp.float32) / (MODES * 4.0 * math.sqrt(MODES))
    shifted = jnp.where(index % 2 == 0, -jnp.roll(flux_modes, -1, axis=-1), jnp.roll(flux_modes, 1, axis=-1))
    return rate * shifted

def reference(velocity, inverses, neighbours, flags):
    basis, weight = basis_table()
    synth = weight[:, None] * basis

    def to_planes(columns_block):
        physical = jnp.einsum('crj,jz->crz', columns_block, synth, precision=highest)
        flux_phys = physical * physical[2:3]
        flux_modes = jnp.einsum('crz,jz->crj', flux_phys, basis, precision=highest) / COEFS
        return spanwise_term(flux_modes)
    blocks = jnp.transpose(velocity.reshape(3, N_PLANE, E_DEV * NODES, COEFS), (1, 0, 2, 3))
    spanwise = jnp.transpose(lax.map(to_planes, blocks), (1, 0, 2, 3)).reshape(velocity.shape)
    point_energy = lax.optimization_barrier(jnp.sum(velocity * velocity * weight, axis=(0, 2)))
    node_energy = point_energy.reshape(ELEMS, NODES)
    node = jnp.arange(NODES, dtype=jnp.int32)
    degree_a = node // (ORDER + 1)
    degree_b = node % (ORDER + 1)
    high_mask = ((degree_a == ORDER) | (degree_b == ORDER)).astype(jnp.float32)
    high = lax.optimization_barrier(jnp.sum(node_energy * high_mask, axis=1))
    total = lax.optimization_barrier(jnp.sum(node_energy, axis=1))
    speed = jnp.sqrt(jnp.sum(total) / (3.0 * NPTS * COEFS))
    sensor = jnp.log10((high + 1e-06) / (total + 1e-06))
    ramp_value = 0.5 * (1.0 + jnp.sin(0.5 * math.pi * jnp.clip(sensor + 2.0, -1.0, 1.0)))
    element_visc = speed * (0.4 * (1.0 + flags.astype(jnp.float32)) * ramp_value)
    element = jnp.arange(ELEMS, dtype=jnp.int32)
    column = element // E_DEV
    offsets = jnp.stack([column - 1, column + 1, column, column], axis=1) * E_DEV
    global_nb = jnp.where(neighbours >= 0, offsets + neighbours, element[:, None]).astype(jnp.int32)
    beside_all = lax.optimization_barrier(jnp.sum(element_visc[global_nb], axis=1))
    viscosity = (2.0 * element_visc + beside_all) / 6.0
    damping = (degree_a * degree_a + degree_b * degree_b).astype(jnp.float32) / (2.0 * ORDER * ORDER)
    point_visc = (viscosity[:, None] * damping[None, :]).reshape(NPTS)
    right_side = velocity - spanwise - point_visc[None, :, None] * velocity
    repeated = jnp.repeat(inverses, 2, axis=0)
    advanced = jnp.einsum('jin,cenj->ceij', repeated, right_side.reshape(3, ELEMS, NODES, COEFS), precision=highest)
    return (advanced.reshape(velocity.shape), viscosity)
```

```python
import math

import jax
import jax.numpy as jnp
import ml_dtypes
import numpy as np
from jax import lax
from jax.experimental import pallas as pl
from jax.experimental.pallas import tpu as pltpu
from jax.sharding import PartitionSpec as P

ORDER = 4
NODES = (ORDER + 1) ** 2
LENGTH = 4.0
LANES = 128
SUB = 8
TILE = SUB * NODES

f32 = jnp.float32
bf16 = jnp.bfloat16

IS_HIGH = [n // (ORDER + 1) == ORDER or n % (ORDER + 1) == ORDER for n in range(NODES)]


def split_np(table):
    high = table.astype(np.float32).astype(ml_dtypes.bfloat16)
    low = (table - high.astype(np.float64)).astype(ml_dtypes.bfloat16)
    return np.stack([high, low])


def tables(coefs):
    modes = coefs // 2
    index = np.arange(coefs)
    pair = index // 2
    odd = index % 2
    freq = np.where(index == 1, modes, pair)
    angle = 2.0 * np.pi * (freq[:, None] * index[None, :] % coefs) / coefs
    use_cos = (odd == 0) | (pair == 0)
    basis = np.where(use_cos[:, None], np.cos(angle), -np.sin(angle))
    weight = np.where(pair == 0, 1.0, 2.0)
    rate = pair / (modes * LENGTH * math.sqrt(modes))
    partner = basis[index ^ 1]
    derive = (np.where(odd == 0, -rate, rate) / coefs)[:, None] * partner
    return split_np(weight[:, None] * basis), split_np(derive.T.copy())


def halves(x):
    high = x.astype(bf16)
    return high, (x - high.astype(f32)).astype(bf16)


def dot(a, b):
    return jnp.dot(a, b, preferred_element_type=f32)


def energy_kernel(first, last, vel_ref, weight_ref, out_ref, point_ref):
    step = pl.program_id(0)
    width = vel_ref.shape[2]
    weight = weight_ref[...]
    acc = None
    for lane in range(0, width, LANES):
        for comp in range(vel_ref.shape[0]):
            x = vel_ref[comp, :, lane : lane + LANES]
            term = x * x * weight[:, lane : lane + LANES]
            acc = term if acc is None else acc + term
    point_ref[...] = acc
    total = jnp.zeros((SUB, LANES), f32)
    high = jnp.zeros((SUB, LANES), f32)
    for n in range(NODES):
        part = point_ref[pl.ds(n, SUB, stride=NODES), :]
        total = total + part
        if IS_HIGH[n]:
            high = high + part
    rows = last - first
    at = pl.multiple_of(rows + step * 2 * SUB, SUB)
    out_ref[pl.ds(at, SUB), :LANES] = total
    out_ref[pl.ds(at + SUB, SUB), :LANES] = high

    @pl.when((step * TILE >= first) & (step * TILE < last))
    def _():
        out_ref[pl.ds(pl.multiple_of(step * TILE - first, SUB), TILE), :] = vel_ref[vel_ref.shape[0] - 1]


def energies(velocity, weight, first, last):
    comps, points, width = velocity.shape
    steps = points // TILE
    rows = last - first + 2 * SUB * steps
    return pl.pallas_call(
        lambda *refs: energy_kernel(first, last, *refs),
        grid=(steps,),
        in_specs=[
            pl.BlockSpec((comps, TILE, width), lambda t: (0, t, 0)),
            pl.BlockSpec((1, width), lambda t: (0, 0)),
        ],
        out_specs=pl.BlockSpec((rows, width), lambda t: (0, 0)),
        out_shape=jax.ShapeDtypeStruct((rows, width), f32),
        scratch_shapes=[pltpu.VMEM((TILE, LANES), f32)],
        compiler_params=pltpu.CompilerParams(vmem_limit_bytes=16 << 20),
        name="energies",
    )(velocity, weight)


def expand_kernel(inv_ref, spread_ref, out_ref):
    spread = spread_ref[...]
    for i in range(NODES):
        x = inv_ref[i]
        high, rest = halves(x)
        mid, low = halves(x - high.astype(f32))
        y = (dot(high, spread) + dot(mid, spread)) + dot(low, spread)
        for t in range(out_ref.shape[0]):
            out_ref[t, i] = y[:, t * LANES : (t + 1) * LANES]


def expand(inverses, width):
    pairs = inverses.shape[0]
    spread = np.repeat(np.eye(pairs), 2, axis=1).astype(ml_dtypes.bfloat16)
    return pl.pallas_call(
        expand_kernel,
        out_shape=jax.ShapeDtypeStruct((width // LANES, NODES, NODES, LANES), f32),
        compiler_params=pltpu.CompilerParams(vmem_limit_bytes=16 << 20),
        name="expand",
    )(jnp.transpose(inverses, (1, 2, 0)), spread)


def chunk_kernel(n_far, is_w, aliased, *refs):
    refs = list(refs)
    own_ref = refs.pop(0)
    far_refs = [refs.pop(0) for _ in range(n_far)]
    wphys_ref = None if is_w else refs.pop(0)
    damp_ref, synth_ref, derive_ref, inv_ref = refs[:4]
    refs = refs[4 + aliased :]
    out_ref = refs.pop(0)
    if is_w:
        wphys_ref = refs.pop(0)
    rhs_ref, res_ref = refs
    width = own_ref.shape[2]
    own = own_ref[0]
    phys = None
    for s, x in enumerate([own] + [r[...] for r in far_refs]):
        high, low = halves(x)
        rows = slice(s * width, (s + 1) * width)
        part = dot(high, synth_ref[0, rows, :])
        part = part + dot(high, synth_ref[1, rows, :])
        part = part + dot(low, synth_ref[0, rows, :])
        phys = part if phys is None else phys + part
    if is_w:
        wphys_ref[...] = phys
        flux = phys * phys
    else:
        flux = phys * wphys_ref[...]
    high, low = halves(flux)
    span = dot(high, derive_ref[0]) + dot(high, derive_ref[1]) + dot(low, derive_ref[0])
    damp = damp_ref[...]
    for t in range(width // LANES):
        lanes = slice(t * LANES, (t + 1) * LANES)
        x = own[:, lanes]
        rhs_ref[t] = x - span[:, lanes] - damp * x

    def solve(t, carry):
        right = [rhs_ref[t, pl.ds(n, SUB, stride=NODES), :] for n in range(NODES)]
        for i in range(NODES):
            acc = None
            for n in range(NODES):
                term = inv_ref[t, i, n : n + 1, :] * right[n]
                acc = term if acc is None else acc + term
            res_ref[t, pl.ds(i, SUB, stride=NODES), :] = acc
        return carry

    lax.fori_loop(0, width // LANES, solve, 0)
    for t in range(width // LANES):
        out_ref[0, :, t * LANES : (t + 1) * LANES] = res_ref[t]


def advance(velocity, far, comp, first, rows, wphys, damp, synth, derive, inv, out):
    comps, points, width = velocity.shape
    coefs = synth.shape[1]
    tiles = width // LANES
    is_w = comp == comps - 1
    at = first // TILE
    whole = lambda shape: pl.BlockSpec(shape, lambda t: (0,) * len(shape), pipeline_mode=pl.Buffered(1))
    row = lambda w: pl.BlockSpec((TILE, w), lambda t: (at + t, 0))
    block = pl.BlockSpec((1, TILE, width), lambda t: (comp, at + t, 0))
    args = [velocity, *far]
    specs = [block] + [pl.BlockSpec((TILE, width), lambda t: (t, 0)) for _ in far]
    if not is_w:
        args.append(wphys)
        specs.append(row(coefs))
    args += [damp, synth, derive, inv]
    specs += [row(LANES), whole(synth.shape), whole(derive.shape), whole(inv.shape)]
    out_shape = [jax.ShapeDtypeStruct(velocity.shape, f32)]
    out_specs = [block]
    aliases = {}
    if out is not None:
        aliases[len(args)] = 0
        args.append(out)
        specs.append(pl.BlockSpec(memory_space=pl.ANY))
    if is_w:
        if wphys is not None:
            aliases[len(args)] = 1
            args.append(wphys)
            specs.append(pl.BlockSpec(memory_space=pl.ANY))
        out_shape.append(jax.ShapeDtypeStruct((points, coefs), f32))
        out_specs.append(row(coefs))
    result = pl.pallas_call(
        lambda *refs: chunk_kernel(len(far), is_w, len(aliases), *refs),
        grid=(rows // TILE,),
        in_specs=specs,
        out_specs=out_specs,
        out_shape=out_shape,
        scratch_shapes=[pltpu.VMEM((tiles, TILE, LANES), f32)] * 2,
        input_output_aliases=aliases,
        compiler_params=pltpu.CompilerParams(vmem_limit_bytes=32 << 20),
        cost_estimate=pl.CostEstimate(
            flops=6 * rows * coefs * (coefs + width), bytes_accessed=8 * rows * width, transcendentals=0
        ),
        name=f"advance_{comp}_{first}",
    )(*args)
    return (result[0], result[1] if is_w else wphys)


def exchange(block):
    count = lax.axis_size("mode")
    return [
        lax.ppermute(block, "mode", [(i, (i + s) % count) for i in range(count)])
        for s in range(1, count)
    ]


def sum_over_plane(value):
    count = lax.axis_size("plane")
    if count & (count - 1):
        return lax.psum(value, "plane")
    step = 1
    while step < count:
        value = value + lax.ppermute(value, "plane", [(i, i ^ step) for i in range(count)])
        step *= 2
    return value


def on_device(velocity, inverses, neighbours, flags):
    mode_count = lax.axis_size("mode")
    plane_count = lax.axis_size("plane")
    mine = lax.axis_index("mode")
    comps, points, width = velocity.shape
    coefs = width * mode_count
    elements = neighbours.shape[0]
    w = comps - 1

    first = velocity[w, :TILE]
    far = {(w, 0, TILE): exchange(first)}
    held, velocity = lax.optimization_barrier((first, velocity))
    index = mine * width + lax.iota(jnp.int32, width)
    weight = jnp.where(index < 2, 1.0, 2.0).astype(f32)[None, :]
    split = 2 * TILE
    packed = energies(velocity, weight, TILE, split)
    packed_far = exchange(packed)
    count = split - TILE
    far[w, TILE, count] = [x[:count] for x in packed_far]
    tail, velocity = lax.optimization_barrier((packed, velocity))
    for comp, begin, rows in (
        [(w, split, points - split)]
        + [(c, 0, points) for c in range(w - 1)]
        + [(w - 1, 0, points // 2 // TILE * TILE)]
        + [(w - 1, r, TILE) for r in range(points // 2 // TILE * TILE, points, TILE)]
    ):
        far[comp, begin, rows] = exchange(velocity[comp, begin : begin + rows])

    parts = jnp.stack([x[count:, :LANES] for x in [packed] + packed_far])
    order = (mine - lax.iota(jnp.int32, mode_count)) % mode_count
    parts = jnp.sum(parts.reshape(mode_count, elements // SUB, 2, SUB, LANES), axis=-1)
    if mode_count == 2:
        sums = parts[0] + parts[1]
    else:
        sums = jnp.sum(jnp.take(parts, order, axis=0), axis=0)
    total = sums[:, 0].reshape(elements)
    high = sums[:, 1].reshape(elements)
    field = sum_over_plane(jnp.sum(total))
    speed = jnp.sqrt(field / (1.0 * comps * points * plane_count * coefs))
    sensor = jnp.log10((high + 1e-06) / (total + 1e-06))
    ramp = 0.5 * (1.0 + jnp.sin(0.5 * math.pi * jnp.clip(sensor + 2.0, -1.0, 1.0)))
    shape = 0.4 * (1.0 + flags.astype(f32)) * ramp
    forward = [(i, i + 1) for i in range(plane_count - 1)]
    west = lax.ppermute(shape, "plane", forward)
    east = lax.ppermute(shape, "plane", [(b, a) for a, b in forward])
    source = speed * shape
    padded = speed * jnp.concatenate([west, shape, east])
    element = lax.iota(jnp.int32, elements)
    base = jnp.array([0, 2 * elements, elements, elements], dtype=jnp.int32)
    target = jnp.where(neighbours >= 0, base[None, :] + neighbours, elements + element[:, None])
    positions = lax.iota(jnp.int32, 3 * elements)
    picked = jnp.where(target[:, :, None] == positions[None, None, :], padded[None, None, :], 0.0)
    beside = jnp.sum(jnp.sum(picked, axis=2), axis=1)
    viscosity = (2.0 * source + beside) / 6.0
    node = np.arange(NODES)
    degrees = (node // (ORDER + 1)) ** 2 + (node % (ORDER + 1)) ** 2
    factor = (degrees / (2.0 * ORDER * ORDER)).astype(np.float32)
    damp = (viscosity[:, None] * factor[None, :]).reshape(points)
    damp = jnp.broadcast_to(damp[:, None], (points, LANES))

    synth_all, derive_all = tables(coefs)
    synth_all = jnp.asarray(synth_all.reshape(2, mode_count, width, coefs))
    synth = jnp.concatenate(
        [lax.dynamic_index_in_dim(synth_all, order[s], 1, keepdims=False) for s in range(mode_count)], axis=1
    )
    derive_all = jnp.asarray(
        np.ascontiguousarray(derive_all.reshape(2, coefs, mode_count, width).transpose(2, 0, 1, 3))
    )
    derive = lax.dynamic_index_in_dim(derive_all, mine, 0, keepdims=False)
    inv = expand(inverses, width)

    out = wphys = None
    for (comp, begin, rows), blocks in far.items():
        out, wphys = advance(
            velocity, blocks, comp, begin, rows, wphys, damp, synth, derive, inv, out
        )
    return (out, viscosity)


def solution(mesh):
    in_specs = (P(None, "plane", "mode"), P("mode", None, None), P("plane", None), P("plane"))
    out_specs = (P(None, "plane", "mode"), P("plane"))
    return jax.shard_map(
        on_device, mesh=mesh, in_specs=in_specs, out_specs=out_specs, check_vma=False
    )
```

```python
import math

import jax
import jax.numpy as jnp
import ml_dtypes
import numpy as np
from jax import lax
from jax.experimental import pallas as pl
from jax.experimental.pallas import tpu as pltpu
from jax.sharding import PartitionSpec as P

ORDER = 4
NODES = (ORDER + 1) ** 2
LENGTH = 4.0
LANES = 128
SUB = 8
TILE = SUB * NODES

f32 = jnp.float32
bf16 = jnp.bfloat16

IS_HIGH = [n // (ORDER + 1) == ORDER or n % (ORDER + 1) == ORDER for n in range(NODES)]


def split_np(table):
    high = table.astype(np.float32).astype(ml_dtypes.bfloat16)
    low = (table - high.astype(np.float64)).astype(ml_dtypes.bfloat16)
    return np.stack([high, low])


def parity_order(width):
    if width == LANES:
        index = np.arange(width)
        return index[index // 2 % 2 == 0], index[index // 2 % 2 == 1]
    index = np.arange(width).reshape(-1, 2, LANES)
    even = index[:, :, np.arange(LANES) // 2 % 2 == 0]
    odd = index[:, ::-1][:, :, np.arange(LANES) // 2 % 2 == 1]
    return even.reshape(-1), odd.reshape(-1)


def tables(coefs, width):
    modes = coefs // 2
    index = np.arange(coefs)
    pair = index // 2
    odd = index % 2
    freq = np.where(index == 1, modes, pair)
    angle = 2.0 * np.pi * (freq[:, None] * index[None, :modes] % coefs) / coefs
    use_cos = (odd == 0) | (pair == 0)
    basis = np.where(use_cos[:, None], np.cos(angle), -np.sin(angle))
    weight = np.where(pair == 0, 1.0, 2.0)
    rate = pair / (modes * LENGTH * math.sqrt(modes))
    partner = basis[index ^ 1]
    derive = (np.where(odd == 0, -rate, rate) / coefs)[:, None] * partner
    groups = coefs // width
    synth = (weight[:, None] * basis).reshape(groups, width, modes)
    derive = derive.reshape(groups, width, modes).transpose(0, 2, 1)
    orders = parity_order(width)
    synth = np.stack([split_np(synth[:, o]) for o in orders])
    derive = [derive[:, :, o] for o in orders]
    if width == LANES:
        derive = [np.pad(derive[p], ((0, 0), (0, 0), (p * LANES // 2, (1 - p) * LANES // 2))) for p in (0, 1)]
    derive = np.stack([split_np(d) for d in derive])
    return np.moveaxis(synth, 2, 0).copy(), np.moveaxis(derive, 2, 0).copy()


def lane_index(shape):
    return lax.broadcasted_iota(jnp.int32, shape, 1)


def take_lanes(x, index):
    return jnp.take_along_axis(x, index, axis=1, mode="promise_in_bounds")


def deinterleave(first, second):
    lane = lane_index(first.shape)
    half = LANES // 2
    low = lane < half
    place = 4 * (lane % half // 2) + lane % 2
    first = take_lanes(first, place + jnp.where(low, 0, 2))
    second = take_lanes(second, place + jnp.where(low, 2, 0))
    return jnp.where(low, first, second), jnp.where(low, second, first)


def interleave(low_part, high_part, flip):
    lane = lane_index(low_part.shape)
    half = LANES // 2
    both = jnp.where(lane < half, low_part, high_part)
    is_odd = lane // 2 % 2
    upper = 1 - is_odd if flip else is_odd
    return take_lanes(both, lane // 4 * 2 + lane % 2 + upper * half)


def halves(x):
    high = x.astype(bf16)
    return high, (x - high.astype(f32)).astype(bf16)


def dot(a, b):
    return jnp.dot(a, b, preferred_element_type=f32)


def energy_kernel(first, last, vel_ref, weight_ref, out_ref, point_ref):
    step = pl.program_id(0)
    width = vel_ref.shape[2]
    weight = weight_ref[...]
    acc = None
    for lane in range(0, width, LANES):
        for comp in range(vel_ref.shape[0]):
            x = vel_ref[comp, :, lane : lane + LANES]
            term = x * x * weight[:, lane : lane + LANES]
            acc = term if acc is None else acc + term
    point_ref[...] = acc
    total = jnp.zeros((SUB, LANES), f32)
    high = jnp.zeros((SUB, LANES), f32)
    for n in range(NODES):
        part = point_ref[pl.ds(n, SUB, stride=NODES), :]
        total = total + part
        if IS_HIGH[n]:
            high = high + part
    rows = last - first

    @pl.when(step == 0)
    def _():
        out_ref[rows:, :] = jnp.zeros((SUB, width), f32)

    lane = lane_index((SUB, LANES))
    held = out_ref[rows:, :LANES]
    held = jnp.where(lane == 2 * step, jnp.sum(total, axis=1, keepdims=True), held)
    held = jnp.where(lane == 2 * step + 1, jnp.sum(high, axis=1, keepdims=True), held)
    out_ref[rows:, :LANES] = held

    @pl.when((step * TILE >= first) & (step * TILE < last))
    def _():
        out_ref[pl.ds(pl.multiple_of(step * TILE - first, SUB), TILE), :] = vel_ref[vel_ref.shape[0] - 1]


def energies(velocity, weight, first, last):
    comps, points, width = velocity.shape
    steps = points // TILE
    rows = last - first + SUB
    return pl.pallas_call(
        lambda *refs: energy_kernel(first, last, *refs),
        grid=(steps,),
        in_specs=[
            pl.BlockSpec((comps, TILE, width), lambda t: (0, t, 0)),
            pl.BlockSpec((1, width), lambda t: (0, 0)),
        ],
        out_specs=pl.BlockSpec((rows, width), lambda t: (0, 0)),
        out_shape=jax.ShapeDtypeStruct((rows, width), f32),
        scratch_shapes=[pltpu.VMEM((TILE, LANES), f32)],
        compiler_params=pltpu.CompilerParams(vmem_limit_bytes=16 << 20),
        name="energies",
    )(velocity, weight)


def expand_kernel(inv_ref, spread_ref, out_ref):
    spread = spread_ref[...]
    for i in range(NODES):
        x = inv_ref[i]
        high, rest = halves(x)
        mid, low = halves(x - high.astype(f32))
        y = (dot(high, spread) + dot(mid, spread)) + dot(low, spread)
        for t in range(out_ref.shape[0]):
            out_ref[t, i] = y[:, t * LANES : (t + 1) * LANES]


def expand(inverses, width):
    pairs = inverses.shape[0]
    spread = np.repeat(np.eye(pairs), 2, axis=1).astype(ml_dtypes.bfloat16)
    return pl.pallas_call(
        expand_kernel,
        out_shape=jax.ShapeDtypeStruct((width // LANES, NODES, NODES, LANES), f32),
        compiler_params=pltpu.CompilerParams(vmem_limit_bytes=16 << 20),
        name="expand",
    )(jnp.transpose(inverses, (1, 2, 0)), spread)


def synthesis(blocks, synth_ref, skip):
    tiles = [x[:, t : t + LANES] for x in blocks for t in range(0, x.shape[1], LANES)]
    pairs = [deinterleave(tiles[t], tiles[t + 1]) for t in range(0, len(tiles), 2)]
    sums = []
    for parity in (0, 1):
        high, low = halves(jnp.concatenate([p[parity] for p in pairs], axis=1))
        rows = slice(skip, skip + high.shape[1])
        first = synth_ref[parity, 0, rows, :]
        sums.append(dot(high, first) + dot(high, synth_ref[parity, 1, rows, :]) + dot(low, first))
    return sums


def early_kernel(own_ref, synth_ref, out_ref):
    modes = out_ref.shape[1] // 2
    out_ref[:, :modes], out_ref[:, modes:] = synthesis([own_ref[0]], synth_ref, 0)


def chunk_kernel(n_far, is_w, is_late, aliased, *refs):
    refs = list(refs)
    own_ref = refs.pop(0)
    far_refs = [refs.pop(0) for _ in range(n_far)]
    early_ref = refs.pop(0) if is_late else None
    wphys_ref = None if is_w else refs.pop(0)
    damp_ref, synth_ref, derive_ref, inv_ref = refs[:4]
    refs = refs[4 + aliased :]
    out_ref = refs.pop(0)
    if is_w:
        wphys_ref = refs.pop(0)
    rhs_ref, res_ref = refs
    width = own_ref.shape[2]
    modes = wphys_ref.shape[1] // 2
    own = own_ref[0]
    far = [r[...] for r in far_refs]
    if is_late:
        even, odd = synthesis(far, synth_ref, width // 2)
        even = even + early_ref[:, :modes]
        odd = odd + early_ref[:, modes:]
    else:
        even, odd = synthesis([own] + far, synth_ref, 0)
    near, away = even + odd, even - odd
    if is_w:
        wphys_ref[:, :modes] = near
        wphys_ref[:, modes:] = away
        near, away = near * near, away * away
    else:
        near, away = near * wphys_ref[:, :modes], away * wphys_ref[:, modes:]
    span = []
    for parity, flux in enumerate((near + away, near - away)):
        high, low = halves(flux)
        first = derive_ref[parity, 0]
        span.append(dot(high, first) + dot(high, derive_ref[parity, 1]) + dot(low, first))
    damp = damp_ref[...]
    for t in range(width // LANES):
        lanes = slice(t * LANES, (t + 1) * LANES)
        if width == LANES:
            term = interleave(span[0], span[1], False)
        else:
            at = slice(t // 2 * LANES, (t // 2 + 1) * LANES)
            term = interleave(span[t % 2][:, at], span[1 - t % 2][:, at], t % 2 == 1)
        x = own[:, lanes]
        rhs_ref[t] = x - term - damp * x

    def solve(t, carry):
        right = [rhs_ref[t, pl.ds(n, SUB, stride=NODES), :] for n in range(NODES)]
        for i in range(NODES):
            acc = [None, None]
            for n in range(NODES):
                term = inv_ref[t, i, n : n + 1, :] * right[n]
                acc[n % 2] = term if n < 2 else acc[n % 2] + term
            res_ref[t, pl.ds(i, SUB, stride=NODES), :] = acc[0] + acc[1]
        return carry

    lax.fori_loop(0, width // LANES, solve, 0)
    for t in range(width // LANES):
        out_ref[0, :, t * LANES : (t + 1) * LANES] = res_ref[t]


def whole(shape):
    return pl.BlockSpec(shape, lambda t: (0,) * len(shape), pipeline_mode=pl.Buffered(1))


def early(velocity, comp, first, rows, synth):
    width = velocity.shape[2]
    coefs = 2 * synth.shape[3]
    return pl.pallas_call(
        early_kernel,
        grid=(rows // TILE,),
        in_specs=[pl.BlockSpec((1, TILE, width), lambda t: (comp, first // TILE + t, 0)), whole(synth.shape)],
        out_specs=pl.BlockSpec((TILE, coefs), lambda t: (t, 0)),
        out_shape=jax.ShapeDtypeStruct((rows, coefs), f32),
        compiler_params=pltpu.CompilerParams(vmem_limit_bytes=16 << 20),
        name="early",
    )(velocity, synth)


def advance(velocity, far, comp, first, rows, ahead, wphys, damp, synth, derive, inv, out):
    comps, points, width = velocity.shape
    coefs = 2 * synth.shape[3]
    tiles = width // LANES
    is_w = comp == comps - 1
    at = first // TILE
    row = lambda w: pl.BlockSpec((TILE, w), lambda t: (at + t, 0))
    block = pl.BlockSpec((1, TILE, width), lambda t: (comp, at + t, 0))
    args = [velocity, *far]
    specs = [block] + [pl.BlockSpec((TILE, width), lambda t: (t, 0)) for _ in far]
    if ahead is not None:
        args.append(ahead)
        specs.append(pl.BlockSpec((TILE, coefs), lambda t: (t, 0)))
    if not is_w:
        args.append(wphys)
        specs.append(row(coefs))
    args += [damp, synth, derive, inv]
    specs += [row(LANES), whole(synth.shape), whole(derive.shape), whole(inv.shape)]
    out_shape = [jax.ShapeDtypeStruct(velocity.shape, f32)]
    out_specs = [block]
    aliases = {}
    if out is not None:
        aliases[len(args)] = 0
        args.append(out)
        specs.append(pl.BlockSpec(memory_space=pl.ANY))
    if is_w:
        if wphys is not None:
            aliases[len(args)] = 1
            args.append(wphys)
            specs.append(pl.BlockSpec(memory_space=pl.ANY))
        out_shape.append(jax.ShapeDtypeStruct((points, coefs), f32))
        out_specs.append(row(coefs))
    result = pl.pallas_call(
        lambda *refs: chunk_kernel(len(far), is_w, ahead is not None, len(aliases), *refs),
        grid=(rows // TILE,),
        in_specs=specs,
        out_specs=out_specs,
        out_shape=out_shape,
        scratch_shapes=[pltpu.VMEM((tiles, TILE, LANES), f32)] * 2,
        input_output_aliases=aliases,
        compiler_params=pltpu.CompilerParams(vmem_limit_bytes=32 << 20),
        cost_estimate=pl.CostEstimate(
            flops=3 * rows * coefs * (coefs + width), bytes_accessed=8 * rows * width, transcendentals=0
        ),
        name=f"advance_{comp}_{first}",
    )(*args)
    return (result[0], result[1] if is_w else wphys)


def exchange(block):
    count = lax.axis_size("mode")
    return [
        lax.ppermute(block, "mode", [(i, (i + s) % count) for i in range(count)])
        for s in range(1, count)
    ]


def sum_over_plane(value):
    count = lax.axis_size("plane")
    if count & (count - 1):
        return lax.psum(value, "plane")
    step = 1
    while step < count:
        value = value + lax.ppermute(value, "plane", [(i, i ^ step) for i in range(count)])
        step *= 2
    return value


def on_device(velocity, inverses, neighbours, flags):
    mode_count = lax.axis_size("mode")
    plane_count = lax.axis_size("plane")
    mine = lax.axis_index("mode")
    comps, points, width = velocity.shape
    coefs = width * mode_count
    elements = neighbours.shape[0]
    w = comps - 1

    first = velocity[w, :TILE]
    far = {(w, 0, TILE): exchange(first)}
    held, velocity = lax.optimization_barrier((first, velocity))
    index = mine * width + lax.iota(jnp.int32, width)
    weight = jnp.where(index < 2, 1.0, 2.0).astype(f32)[None, :]
    split = 2 * TILE
    packed = energies(velocity, weight, TILE, split)
    packed_far = exchange(packed)
    count = split - TILE
    far[w, TILE, count] = [x[:count] for x in packed_far]
    tail, velocity = lax.optimization_barrier((packed, velocity))
    for comp, begin, rows in (
        [(w, split, points - split)]
        + [(c, 0, points) for c in range(w - 1)]
        + [(w - 1, 0, points // 2 // TILE * TILE)]
        + [(w - 1, r, TILE) for r in range(points // 2 // TILE * TILE, points, TILE)]
    ):
        far[comp, begin, rows] = exchange(velocity[comp, begin : begin + rows])

    steps = points // TILE
    parts = jnp.stack([x[count:, : 2 * steps] for x in [packed] + packed_far])
    order = (mine - lax.iota(jnp.int32, mode_count)) % mode_count
    if mode_count == 2:
        sums = parts[0] + parts[1]
    else:
        sums = jnp.sum(jnp.take(parts, order, axis=0), axis=0)
    sums = jnp.transpose(sums.reshape(SUB, steps, 2), (2, 1, 0)).reshape(2, elements)
    total, high = sums[0], sums[1]
    field = sum_over_plane(jnp.sum(total))
    speed = jnp.sqrt(field / (1.0 * comps * points * plane_count * coefs))
    sensor = jnp.log10((high + 1e-06) / (total + 1e-06))
    ramp = 0.5 * (1.0 + jnp.sin(0.5 * math.pi * jnp.clip(sensor + 2.0, -1.0, 1.0)))
    shape = 0.4 * (1.0 + flags.astype(f32)) * ramp
    forward = [(i, i + 1) for i in range(plane_count - 1)]
    west = lax.ppermute(shape, "plane", forward)
    east = lax.ppermute(shape, "plane", [(b, a) for a, b in forward])
    source = speed * shape
    padded = speed * jnp.concatenate([west, shape, east])
    element = lax.iota(jnp.int32, elements)
    base = jnp.array([0, 2 * elements, elements, elements], dtype=jnp.int32)
    target = jnp.where(neighbours >= 0, base[None, :] + neighbours, elements + element[:, None])
    positions = lax.iota(jnp.int32, 3 * elements)
    picked = jnp.where(target[:, :, None] == positions[None, None, :], padded[None, None, :], 0.0)
    beside = jnp.sum(jnp.sum(picked, axis=2), axis=1)
    viscosity = (2.0 * source + beside) / 6.0
    node = np.arange(NODES)
    degrees = (node // (ORDER + 1)) ** 2 + (node % (ORDER + 1)) ** 2
    factor = (degrees / (2.0 * ORDER * ORDER)).astype(np.float32)
    damp = (viscosity[:, None] * factor[None, :]).reshape(points)
    damp = jnp.broadcast_to(damp[:, None], (points, LANES))

    synth_all, derive_all = tables(coefs, width)
    pick = lambda s: lax.dynamic_index_in_dim(jnp.asarray(synth_all), order[s], 0, keepdims=False)
    blocks = [pick(s) for s in range(mode_count)]
    swapped = blocks if width > LANES else [blocks[s ^ 1] for s in range(mode_count)]
    synth = jnp.stack(
        [jnp.concatenate([b[p] for b in group], axis=1) for p, group in enumerate((blocks, swapped))]
    )
    derive = lax.dynamic_index_in_dim(jnp.asarray(derive_all), mine, 0, keepdims=False)
    inv = expand(inverses, width)

    out = wphys = None
    for place, (comp, begin, rows) in enumerate(far):
        ahead = None
        if place == len(far) - 1 and width > LANES:
            ahead = early(velocity, comp, begin, rows, synth)
        out, wphys = advance(
            velocity, far[comp, begin, rows], comp, begin, rows, ahead, wphys, damp, synth, derive, inv, out
        )
    return (out, viscosity)


def solution(mesh):
    in_specs = (P(None, "plane", "mode"), P("mode", None, None), P("plane", None), P("plane"))
    out_specs = (P(None, "plane", "mode"), P("plane"))
    return jax.shard_map(
        on_device, mesh=mesh, in_specs=in_specs, out_specs=out_specs, check_vma=False
    )
```

```python
import math

import jax
import jax.numpy as jnp
import ml_dtypes
import numpy as np
from jax import lax
from jax.experimental import pallas as pl
from jax.experimental.pallas import tpu as pltpu
from jax.sharding import PartitionSpec as P

ORDER = 4
NODES = (ORDER + 1) ** 2
LENGTH = 4.0
LANES = 128
SUB = 8
TILE = SUB * NODES

f32 = jnp.float32
bf16 = jnp.bfloat16

IS_HIGH = [n // (ORDER + 1) == ORDER or n % (ORDER + 1) == ORDER for n in range(NODES)]


def split_np(table):
    high = table.astype(np.float32).astype(ml_dtypes.bfloat16)
    low = (table - high.astype(np.float64)).astype(ml_dtypes.bfloat16)
    return np.stack([high, low])


def parity_order(width):
    if width == LANES:
        index = np.arange(width)
        return index[index // 2 % 2 == 0], index[index // 2 % 2 == 1]
    index = np.arange(width).reshape(-1, 2, LANES)
    even = index[:, :, np.arange(LANES) // 2 % 2 == 0]
    odd = index[:, ::-1][:, :, np.arange(LANES) // 2 % 2 == 1]
    return even.reshape(-1), odd.reshape(-1)


def tables(coefs, width):
    modes = coefs // 2
    index = np.arange(coefs)
    pair = index // 2
    odd = index % 2
    freq = np.where(index == 1, modes, pair)
    angle = 2.0 * np.pi * (freq[:, None] * index[None, :modes] % coefs) / coefs
    use_cos = (odd == 0) | (pair == 0)
    basis = np.where(use_cos[:, None], np.cos(angle), -np.sin(angle))
    weight = np.where(pair == 0, 1.0, 2.0)
    rate = pair / (modes * LENGTH * math.sqrt(modes))
    partner = basis[index ^ 1]
    derive = (np.where(odd == 0, -rate, rate) / coefs)[:, None] * partner
    groups = coefs // width
    synth = (weight[:, None] * basis).reshape(groups, width, modes)
    derive = derive.reshape(groups, width, modes).transpose(0, 2, 1)
    orders = parity_order(width)
    synth = np.stack([split_np(synth[:, o]) for o in orders])
    derive = [derive[:, :, o] for o in orders]
    if width == LANES:
        derive = [np.pad(derive[p], ((0, 0), (0, 0), (p * LANES // 2, (1 - p) * LANES // 2))) for p in (0, 1)]
    derive = np.stack([split_np(d) for d in derive])
    return np.moveaxis(synth, 2, 0).copy(), np.moveaxis(derive, 2, 0).copy()


def lane_index(shape):
    return lax.broadcasted_iota(jnp.int32, shape, 1)


def take_lanes(x, index):
    return jnp.take_along_axis(x, index, axis=1, mode="promise_in_bounds")


def deinterleave(first, second):
    lane = lane_index(first.shape)
    half = LANES // 2
    low = lane < half
    place = 4 * (lane % half // 2) + lane % 2
    first = take_lanes(first, place + jnp.where(low, 0, 2))
    second = take_lanes(second, place + jnp.where(low, 2, 0))
    return jnp.where(low, first, second), jnp.where(low, second, first)


def interleave(low_part, high_part, flip):
    lane = lane_index(low_part.shape)
    half = LANES // 2
    both = jnp.where(lane < half, low_part, high_part)
    is_odd = lane // 2 % 2
    upper = 1 - is_odd if flip else is_odd
    return take_lanes(both, lane // 4 * 2 + lane % 2 + upper * half)


def halves(x):
    high = x.astype(bf16)
    return high, (x - high.astype(f32)).astype(bf16)


def dot(a, b):
    return jnp.dot(a, b, preferred_element_type=f32)


def first_kernel(at_ref, vel_ref, weight_ref, energy_ref, rest_ref, point_ref):
    step = pl.program_id(0)
    comps, _, width = vel_ref.shape
    weight = weight_ref[...]
    acc = None
    for lane in range(0, width, LANES):
        for comp in range(comps):
            x = vel_ref[comp, :, lane : lane + LANES]
            term = x * x * weight[:, lane : lane + LANES]
            acc = term if acc is None else acc + term
    point_ref[...] = acc
    total = jnp.zeros((SUB, LANES), f32)
    high = jnp.zeros((SUB, LANES), f32)
    for n in range(NODES):
        part = point_ref[pl.ds(n, SUB, stride=NODES), :]
        total = total + part
        if IS_HIGH[n]:
            high = high + part

    @pl.when(step == 0)
    def _():
        energy_ref[...] = jnp.zeros(energy_ref.shape, f32)

    here = lane_index((SUB, LANES)) == step
    for q, part in enumerate((total, high)):
        energy_ref[q] = jnp.where(here, jnp.sum(part, axis=1, keepdims=True), energy_ref[q])

    @pl.when(step > 0)
    def _():
        rest_ref[pl.ds(pl.multiple_of((step - 1) * TILE, SUB), TILE), :] = vel_ref[comps - 1]

    @pl.when(step == at_ref[0])
    def _():
        rest_ref[rest_ref.shape[0] - TILE :, :] = vel_ref[comps - 2]


def first_pass(velocity, weight, there, lend):
    comps, points, width = velocity.shape
    shape = (2, SUB, LANES)
    rest = points if lend else points - TILE
    return pl.pallas_call(
        first_kernel,
        grid_spec=pltpu.PrefetchScalarGridSpec(
            num_scalar_prefetch=1,
            grid=(points // TILE,),
            in_specs=[
                pl.BlockSpec((comps, TILE, width), lambda t, at: (0, t, 0)),
                pl.BlockSpec((1, width), lambda t, at: (0, 0)),
            ],
            out_specs=[
                pl.BlockSpec(shape, lambda t, at: (0, 0, 0)),
                pl.BlockSpec((rest, width), lambda t, at: (0, 0)),
            ],
            scratch_shapes=[pltpu.VMEM((TILE, LANES), f32)],
        ),
        out_shape=[jax.ShapeDtypeStruct(shape, f32), jax.ShapeDtypeStruct((rest, width), f32)],
        compiler_params=pltpu.CompilerParams(vmem_limit_bytes=16 << 20),
        name="first_pass",
    )(there, velocity, weight)


def expand_kernel(inv_ref, spread_ref, out_ref):
    spread = spread_ref[...]
    for i in range(NODES):
        x = inv_ref[i]
        high, rest = halves(x)
        mid, low = halves(x - high.astype(f32))
        y = (dot(high, spread) + dot(mid, spread)) + dot(low, spread)
        for t in range(out_ref.shape[0]):
            out_ref[t, i] = y[:, t * LANES : (t + 1) * LANES]


def expand(inverses, width):
    pairs = inverses.shape[0]
    spread = np.repeat(np.eye(pairs), 2, axis=1).astype(ml_dtypes.bfloat16)
    return pl.pallas_call(
        expand_kernel,
        out_shape=jax.ShapeDtypeStruct((width // LANES, NODES, NODES, LANES), f32),
        compiler_params=pltpu.CompilerParams(vmem_limit_bytes=16 << 20),
        name="expand",
    )(jnp.transpose(inverses, (1, 2, 0)), spread)


def synthesis(blocks, synth_ref):
    tiles = [x[:, t : t + LANES] for x in blocks for t in range(0, x.shape[1], LANES)]
    pairs = [deinterleave(tiles[t], tiles[t + 1]) for t in range(0, len(tiles), 2)]
    sums = []
    for parity in (0, 1):
        high, low = halves(jnp.concatenate([p[parity] for p in pairs], axis=1))
        first = synth_ref[parity, 0]
        sums.append(dot(high, first) + dot(high, synth_ref[parity, 1]) + dot(low, first))
    return sums


def spanwise(near, away, width, derive_refs):
    parts = [halves(near + away), halves(near - away)]
    groups = []
    for derive_ref in derive_refs:
        span = []
        for parity, (high, low) in enumerate(parts):
            first = derive_ref[parity, 0]
            span.append(dot(high, first) + dot(high, derive_ref[parity, 1]) + dot(low, first))
        if width == LANES:
            groups.append([interleave(span[0], span[1], False)])
            continue
        tiles = []
        for t in range(width // LANES):
            at = slice(t // 2 * LANES, (t // 2 + 1) * LANES)
            tiles.append(interleave(span[t % 2][:, at], span[1 - t % 2][:, at], t % 2 == 1))
        groups.append(tiles)
    return groups


def element_solve(rhs_ref, res_ref, inv_ref):
    def solve(t, carry):
        right = [rhs_ref[t, pl.ds(n, SUB, stride=NODES), :] for n in range(NODES)]
        for i in range(NODES):
            acc = [None, None]
            for n in range(NODES):
                term = inv_ref[t, i, n : n + 1, :] * right[n]
                acc[n % 2] = term if n < 2 else acc[n % 2] + term
            res_ref[t, pl.ds(i, SUB, stride=NODES), :] = acc[0] + acc[1]
        return carry

    lax.fori_loop(0, inv_ref.shape[0], solve, 0)


def chunk_kernel(n_far, is_w, aliased, *refs):
    refs = list(refs)
    own_ref = refs.pop(0)
    far_refs = [refs.pop(0) for _ in range(n_far)]
    wphys_ref = None if is_w else refs.pop(0)
    damp_ref, synth_ref, derive_ref, inv_ref = refs[:4]
    refs = refs[4 + aliased :]
    out_ref = refs.pop(0)
    if is_w:
        wphys_ref = refs.pop(0)
    rhs_ref, res_ref = refs
    width = own_ref.shape[2]
    modes = wphys_ref.shape[1] // 2
    own = own_ref[0]
    even, odd = synthesis([own] + [r[...] for r in far_refs], synth_ref)
    near, away = even + odd, even - odd
    if is_w:
        wphys_ref[:, :modes] = near
        wphys_ref[:, modes:] = away
        near, away = near * near, away * away
    else:
        near, away = near * wphys_ref[:, :modes], away * wphys_ref[:, modes:]
    damp = damp_ref[...]
    for t, term in enumerate(spanwise(near, away, width, [derive_ref])[0]):
        x = own[:, t * LANES : (t + 1) * LANES]
        rhs_ref[t] = x - term - damp * x
    element_solve(rhs_ref, res_ref, inv_ref)
    for t in range(width // LANES):
        out_ref[0, :, t * LANES : (t + 1) * LANES] = res_ref[t]


def whole(shape):
    return pl.BlockSpec(shape, lambda *t: (0,) * len(shape), pipeline_mode=pl.Buffered(1))


def advance(velocity, far, comp, first, rows, wphys, damp, synth, derive, inv, out):
    comps, points, width = velocity.shape
    coefs = 2 * synth.shape[3]
    tiles = width // LANES
    is_w = comp == comps - 1
    at = first // TILE
    row = lambda w: pl.BlockSpec((TILE, w), lambda t: (at + t, 0))
    block = pl.BlockSpec((1, TILE, width), lambda t: (comp, at + t, 0))
    args = [velocity, *far]
    specs = [block] + [pl.BlockSpec((TILE, width), lambda t: (t, 0)) for _ in far]
    if not is_w:
        args.append(wphys)
        specs.append(row(coefs))
    args += [damp, synth, derive, inv]
    specs += [row(LANES), whole(synth.shape), whole(derive.shape), whole(inv.shape)]
    out_shape = [jax.ShapeDtypeStruct(velocity.shape, f32)]
    out_specs = [block]
    aliases = {}
    if out is not None:
        aliases[len(args)] = 0
        args.append(out)
        specs.append(pl.BlockSpec(memory_space=pl.ANY))
    if is_w:
        if wphys is not None:
            aliases[len(args)] = 1
            args.append(wphys)
            specs.append(pl.BlockSpec(memory_space=pl.ANY))
        out_shape.append(jax.ShapeDtypeStruct((points, coefs), f32))
        out_specs.append(row(coefs))
    result = pl.pallas_call(
        lambda *refs: chunk_kernel(len(far), is_w, len(aliases), *refs),
        grid=(rows // TILE,),
        in_specs=specs,
        out_specs=out_specs,
        out_shape=out_shape,
        scratch_shapes=[pltpu.VMEM((tiles, TILE, LANES), f32)] * 2,
        input_output_aliases=aliases,
        compiler_params=pltpu.CompilerParams(vmem_limit_bytes=20 << 20),
        cost_estimate=pl.CostEstimate(
            flops=3 * rows * coefs * (coefs + width), bytes_accessed=8 * rows * width, transcendentals=0
        ),
        name=f"advance_{comp}_{first}",
    )(*args)
    return (result[0], result[1] if is_w else wphys)


def both_kernel(at_ref, own_ref, far_ref, wphys_ref, synth_ref, derive_ref, other_ref, span_ref, back_ref):
    modes = wphys_ref.shape[1] // 2
    width = far_ref.shape[1]
    even, odd = synthesis([own_ref[0], far_ref[...]], synth_ref)
    near = (even + odd) * wphys_ref[:, :modes]
    away = (even - odd) * wphys_ref[:, modes:]
    groups = spanwise(near, away, width, [derive_ref, other_ref])
    for ref, tiles in zip((span_ref, back_ref), groups):
        for t, term in enumerate(tiles):
            ref[:, t * LANES : (t + 1) * LANES] = term


def both_groups(velocity, comp, at, far, wphys, synth, derive, other):
    width = velocity.shape[2]
    last = far.shape[0] // TILE - 1
    return pl.pallas_call(
        both_kernel,
        grid_spec=pltpu.PrefetchScalarGridSpec(
            num_scalar_prefetch=1,
            grid=(1,),
            in_specs=[
                pl.BlockSpec((1, TILE, width), lambda t, at: (comp, at[0], 0)),
                pl.BlockSpec((TILE, width), lambda t, at: (last, 0)),
                pl.BlockSpec((TILE, wphys.shape[1]), lambda t, at: (at[0], 0)),
                whole(synth.shape),
                whole(derive.shape),
                whole(other.shape),
            ],
            out_specs=[pl.BlockSpec((TILE, width), lambda t, at: (0, 0))] * 2,
        ),
        out_shape=[jax.ShapeDtypeStruct((TILE, width), f32)] * 2,
        compiler_params=pltpu.CompilerParams(vmem_limit_bytes=20 << 20),
        name="both_groups",
    )(at, velocity, far, wphys, synth, derive, other)


def finish_kernel(at_ref, own_ref, span_ref, damp_ref, inv_ref, held_ref, out_ref, rhs_ref, res_ref):
    damp = damp_ref[...]
    for t in range(inv_ref.shape[0]):
        lanes = slice(t * LANES, (t + 1) * LANES)
        x = own_ref[0, :, lanes]
        rhs_ref[t] = x - span_ref[:, lanes] - damp * x
    element_solve(rhs_ref, res_ref, inv_ref)
    for t in range(inv_ref.shape[0]):
        out_ref[0, :, t * LANES : (t + 1) * LANES] = res_ref[t]


def finish(velocity, comp, at, span, damp, inv, out, name):
    width = velocity.shape[2]
    block = pl.BlockSpec((1, TILE, width), lambda t, at: (comp, at[0], 0))
    return pl.pallas_call(
        finish_kernel,
        grid_spec=pltpu.PrefetchScalarGridSpec(
            num_scalar_prefetch=1,
            grid=(1,),
            in_specs=[
                block,
                pl.BlockSpec((TILE, width), lambda t, at: (0, 0)),
                pl.BlockSpec((TILE, LANES), lambda t, at: (at[0], 0)),
                whole(inv.shape),
                pl.BlockSpec(memory_space=pl.ANY),
            ],
            out_specs=block,
            scratch_shapes=[pltpu.VMEM((width // LANES, TILE, LANES), f32)] * 2,
        ),
        out_shape=jax.ShapeDtypeStruct(velocity.shape, f32),
        input_output_aliases={5: 0},
        compiler_params=pltpu.CompilerParams(vmem_limit_bytes=8 << 20),
        name=name,
    )(at, velocity, span, damp, inv, out)


def exchange(block):
    count = lax.axis_size("mode")
    return [
        lax.ppermute(block, "mode", [(i, (i + s) % count) for i in range(count)])
        for s in range(1, count)
    ]


def sum_over_plane(value):
    count = lax.axis_size("plane")
    if count & (count - 1):
        return lax.psum(value, "plane")
    step = 1
    while step < count:
        value = value + lax.ppermute(value, "plane", [(i, i ^ step) for i in range(count)])
        step *= 2
    return value


def on_device(velocity, inverses, neighbours, flags):
    mode_count = lax.axis_size("mode")
    plane_count = lax.axis_size("plane")
    mine = lax.axis_index("mode")
    comps, points, width = velocity.shape
    coefs = width * mode_count
    elements = neighbours.shape[0]
    w = comps - 1

    first = velocity[w, :TILE]
    far = {(w, 0, TILE): exchange(first)}
    held, velocity = lax.optimization_barrier((first, velocity))
    index = mine * width + lax.iota(jnp.int32, width)
    weight = jnp.where(index < 2, 1.0, 2.0).astype(f32)[None, :]
    blocks = points // TILE
    shared = mode_count == 2 and width > LANES and blocks > 2
    here = jnp.reshape(blocks - 2 + mine, (1,))
    there = jnp.reshape(blocks - 1 - mine if shared else -1, (1,))
    packed, rest = first_pass(velocity, weight, there, shared)
    packed_far = exchange(packed)
    far[w, TILE, points - TILE] = exchange(rest)
    tail, velocity = lax.optimization_barrier((packed, velocity))
    for comp in range(w - 1):
        far[comp, 0, points] = exchange(velocity[comp])
    stop = points - 2 * TILE if shared else points
    for begin in range(0, stop, TILE):
        far[w - 1, begin, TILE] = exchange(velocity[w - 1, begin : begin + TILE])

    steps = points // TILE
    parts = jnp.stack([x[:, :, :steps] for x in [packed] + packed_far])
    order = (mine - lax.iota(jnp.int32, mode_count)) % mode_count
    if mode_count == 2:
        sums = parts[0] + parts[1]
    else:
        sums = jnp.sum(jnp.take(parts, order, axis=0), axis=0)
    sums = jnp.transpose(sums, (0, 2, 1)).reshape(2, elements)
    total, high = sums[0], sums[1]
    field = sum_over_plane(jnp.sum(total))
    speed = jnp.sqrt(field / (1.0 * comps * points * plane_count * coefs))
    sensor = jnp.log10((high + 1e-06) / (total + 1e-06))
    ramp = 0.5 * (1.0 + jnp.sin(0.5 * math.pi * jnp.clip(sensor + 2.0, -1.0, 1.0)))
    shape = 0.4 * (1.0 + flags.astype(f32)) * ramp
    forward = [(i, i + 1) for i in range(plane_count - 1)]
    west = lax.ppermute(shape, "plane", forward)
    east = lax.ppermute(shape, "plane", [(b, a) for a, b in forward])
    source = speed * shape
    padded = speed * jnp.concatenate([west, shape, east])
    element = lax.iota(jnp.int32, elements)
    base = jnp.array([0, 2 * elements, elements, elements], dtype=jnp.int32)
    target = jnp.where(neighbours >= 0, base[None, :] + neighbours, elements + element[:, None])
    positions = lax.iota(jnp.int32, 3 * elements)
    picked = jnp.where(target[:, :, None] == positions[None, None, :], padded[None, None, :], 0.0)
    beside = jnp.sum(jnp.sum(picked, axis=2), axis=1)
    viscosity = (2.0 * source + beside) / 6.0
    node = np.arange(NODES)
    degrees = (node // (ORDER + 1)) ** 2 + (node % (ORDER + 1)) ** 2
    factor = (degrees / (2.0 * ORDER * ORDER)).astype(np.float32)
    damp = (viscosity[:, None] * factor[None, :]).reshape(points)
    damp = jnp.broadcast_to(damp[:, None], (points, LANES))

    synth_all, derive_all = (jnp.asarray(x) for x in tables(coefs, width))
    group = lambda table, at: lax.dynamic_index_in_dim(table, at, 0, keepdims=False)
    rows = [group(synth_all, order[s]) for s in range(mode_count)]
    swapped = rows if width > LANES else [rows[s ^ 1] for s in range(mode_count)]
    synth = jnp.stack([jnp.concatenate([x[p] for x in part], axis=1) for p, part in enumerate((rows, swapped))])
    derive = group(derive_all, mine)
    inv = expand(inverses, width)

    out = wphys = back = None
    for (comp, begin, count), blocks in far.items():
        if shared and back is None and comp != w:
            lent = far[w, TILE, points - TILE][0]
            span, back = both_groups(velocity, w - 1, here, lent, wphys, synth, derive, group(derive_all, 1 - mine))
            back = exchange(back)[0]
        out, wphys = advance(velocity, blocks, comp, begin, count, wphys, damp, synth, derive, inv, out)
    if shared:
        out = finish(velocity, w - 1, here, span, damp, inv, out, "finish_here")
        out = finish(velocity, w - 1, there, back, damp, inv, out, "finish_there")
    return (out, viscosity)


def solution(mesh):
    in_specs = (P(None, "plane", "mode"), P("mode", None, None), P("plane", None), P("plane"))
    out_specs = (P(None, "plane", "mode"), P("plane"))
    return jax.shard_map(
        on_device, mesh=mesh, in_specs=in_specs, out_specs=out_specs, check_vma=False
    )
```

```python
import math

import jax
import jax.numpy as jnp
import ml_dtypes
import numpy as np
from jax import lax
from jax.experimental import pallas as pl
from jax.experimental.pallas import tpu as pltpu
from jax.sharding import PartitionSpec as P

ORDER = 4
NODES = (ORDER + 1) ** 2
LENGTH = 4.0
LANES = 128
SUB = 8
TILE = SUB * NODES

f32 = jnp.float32
bf16 = jnp.bfloat16

IS_HIGH = [n // (ORDER + 1) == ORDER or n % (ORDER + 1) == ORDER for n in range(NODES)]


def split_np(table):
    high = table.astype(np.float32).astype(ml_dtypes.bfloat16)
    low = (table - high.astype(np.float64)).astype(ml_dtypes.bfloat16)
    return np.stack([high, low])


def parity_order(width):
    if width == LANES:
        index = np.arange(width)
        return index[index // 2 % 2 == 0], index[index // 2 % 2 == 1]
    index = np.arange(width).reshape(-1, 2, LANES)
    even = index[:, :, np.arange(LANES) // 2 % 2 == 0]
    odd = index[:, ::-1][:, :, np.arange(LANES) // 2 % 2 == 1]
    return even.reshape(-1), odd.reshape(-1)


def tables(coefs, width):
    modes = coefs // 2
    index = np.arange(coefs)
    pair = index // 2
    odd = index % 2
    freq = np.where(index == 1, modes, pair)
    angle = 2.0 * np.pi * (freq[:, None] * index[None, :modes] % coefs) / coefs
    use_cos = (odd == 0) | (pair == 0)
    basis = np.where(use_cos[:, None], np.cos(angle), -np.sin(angle))
    weight = np.where(pair == 0, 1.0, 2.0)
    rate = pair / (modes * LENGTH * math.sqrt(modes))
    partner = basis[index ^ 1]
    derive = (np.where(odd == 0, -rate, rate) / coefs)[:, None] * partner
    groups = coefs // width
    synth = (weight[:, None] * basis).reshape(groups, width, modes)
    derive = derive.reshape(groups, width, modes).transpose(0, 2, 1)
    orders = parity_order(width)
    synth = np.stack([split_np(synth[:, o]) for o in orders])
    derive = [derive[:, :, o] for o in orders]
    if width == LANES:
        derive = [np.pad(derive[p], ((0, 0), (0, 0), (p * LANES // 2, (1 - p) * LANES // 2))) for p in (0, 1)]
    derive = np.stack([split_np(d) for d in derive])
    return np.moveaxis(synth, 2, 0).copy(), np.moveaxis(derive, 2, 0).copy()


def lane_index(shape):
    return lax.broadcasted_iota(jnp.int32, shape, 1)


def take_lanes(x, index):
    return jnp.take_along_axis(x, index, axis=1, mode="promise_in_bounds")


def deinterleave(first, second):
    lane = lane_index(first.shape)
    half = LANES // 2
    low = lane < half
    place = 4 * (lane % half // 2) + lane % 2
    first = take_lanes(first, place + jnp.where(low, 0, 2))
    second = take_lanes(second, place + jnp.where(low, 2, 0))
    return jnp.where(low, first, second), jnp.where(low, second, first)


def interleave(low_part, high_part, flip):
    lane = lane_index(low_part.shape)
    half = LANES // 2
    both = jnp.where(lane < half, low_part, high_part)
    is_odd = lane // 2 % 2
    upper = 1 - is_odd if flip else is_odd
    return take_lanes(both, lane // 4 * 2 + lane % 2 + upper * half)


def halves(x):
    high = x.astype(bf16)
    return high, (x - high.astype(f32)).astype(bf16)


def dot(a, b):
    return jnp.dot(a, b, preferred_element_type=f32)


def first_kernel(at_ref, vel_ref, weight_ref, energy_ref, rest_ref, point_ref):
    step = pl.program_id(0)
    comps, _, width = vel_ref.shape
    weight = weight_ref[...]
    acc = None
    for lane in range(0, width, LANES):
        for comp in range(comps):
            x = vel_ref[comp, :, lane : lane + LANES]
            term = x * x * weight[:, lane : lane + LANES]
            acc = term if acc is None else acc + term
    point_ref[...] = acc
    total = jnp.zeros((SUB, LANES), f32)
    high = jnp.zeros((SUB, LANES), f32)
    for n in range(NODES):
        part = point_ref[pl.ds(n, SUB, stride=NODES), :]
        total = total + part
        if IS_HIGH[n]:
            high = high + part

    @pl.when(step == 0)
    def _():
        energy_ref[...] = jnp.zeros(energy_ref.shape, f32)

    here = lane_index((SUB, LANES)) == step
    for q, part in enumerate((total, high)):
        energy_ref[q] = jnp.where(here, jnp.sum(part, axis=1, keepdims=True), energy_ref[q])

    @pl.when(step > 0)
    def _():
        rest_ref[pl.ds(pl.multiple_of((step - 1) * TILE, SUB), TILE), :] = vel_ref[comps - 1]

    @pl.when(step == at_ref[0])
    def _():
        rest_ref[rest_ref.shape[0] - TILE :, :] = vel_ref[comps - 2]


def first_pass(velocity, weight, there, lend):
    comps, points, width = velocity.shape
    shape = (2, SUB, LANES)
    rest = points if lend else points - TILE
    return pl.pallas_call(
        first_kernel,
        grid_spec=pltpu.PrefetchScalarGridSpec(
            num_scalar_prefetch=1,
            grid=(points // TILE,),
            in_specs=[
                pl.BlockSpec((comps, TILE, width), lambda t, at: (0, t, 0)),
                pl.BlockSpec((1, width), lambda t, at: (0, 0)),
            ],
            out_specs=[
                pl.BlockSpec(shape, lambda t, at: (0, 0, 0)),
                pl.BlockSpec((rest, width), lambda t, at: (0, 0)),
            ],
            scratch_shapes=[pltpu.VMEM((TILE, LANES), f32)],
        ),
        out_shape=[jax.ShapeDtypeStruct(shape, f32), jax.ShapeDtypeStruct((rest, width), f32)],
        compiler_params=pltpu.CompilerParams(vmem_limit_bytes=16 << 20),
        name="first_pass",
    )(there, velocity, weight)


def expand_kernel(inv_ref, spread_ref, out_ref):
    spread = spread_ref[...]
    for i in range(NODES):
        x = inv_ref[i]
        high, rest = halves(x)
        mid, low = halves(x - high.astype(f32))
        y = (dot(high, spread) + dot(mid, spread)) + dot(low, spread)
        for t in range(out_ref.shape[0]):
            out_ref[t, i] = y[:, t * LANES : (t + 1) * LANES]


def expand(inverses, width):
    pairs = inverses.shape[0]
    spread = np.repeat(np.eye(pairs), 2, axis=1).astype(ml_dtypes.bfloat16)
    return pl.pallas_call(
        expand_kernel,
        out_shape=jax.ShapeDtypeStruct((width // LANES, NODES, NODES, LANES), f32),
        compiler_params=pltpu.CompilerParams(vmem_limit_bytes=16 << 20),
        name="expand",
    )(jnp.transpose(inverses, (1, 2, 0)), spread)


def synthesis(blocks, synth_ref):
    tiles = [x[:, t : t + LANES] for x in blocks for t in range(0, x.shape[1], LANES)]
    pairs = [deinterleave(tiles[t], tiles[t + 1]) for t in range(0, len(tiles), 2)]
    sums = []
    for parity in (0, 1):
        high, low = halves(jnp.concatenate([p[parity] for p in pairs], axis=1))
        first = synth_ref[parity, 0]
        sums.append(dot(high, first) + dot(high, synth_ref[parity, 1]) + dot(low, first))
    return sums


def spanwise(near, away, width, derive_refs):
    parts = [halves(near + away), halves(near - away)]
    groups = []
    for derive_ref in derive_refs:
        span = []
        for parity, (high, low) in enumerate(parts):
            first = derive_ref[parity, 0]
            span.append(dot(high, first) + dot(high, derive_ref[parity, 1]) + dot(low, first))
        if width == LANES:
            groups.append([interleave(span[0], span[1], False)])
            continue
        tiles = []
        for t in range(width // LANES):
            at = slice(t // 2 * LANES, (t // 2 + 1) * LANES)
            tiles.append(interleave(span[t % 2][:, at], span[1 - t % 2][:, at], t % 2 == 1))
        groups.append(tiles)
    return groups


def element_solve(rhs_ref, res_ref, inv_ref):
    def solve(t, carry):
        right = [rhs_ref[t, pl.ds(n, SUB, stride=NODES), :] for n in range(NODES)]
        for i in range(NODES):
            acc = [None, None]
            for n in range(NODES):
                term = inv_ref[t, i, n : n + 1, :] * right[n]
                acc[n % 2] = term if n < 2 else acc[n % 2] + term
            res_ref[t, pl.ds(i, SUB, stride=NODES), :] = acc[0] + acc[1]
        return carry

    lax.fori_loop(0, inv_ref.shape[0], solve, 0)


def chunk_kernel(n_far, is_w, aliased, *refs):
    refs = list(refs)
    own_ref = refs.pop(0)
    far_refs = [refs.pop(0) for _ in range(n_far)]
    wphys_ref = None if is_w else refs.pop(0)
    damp_ref, synth_ref, derive_ref, inv_ref = refs[:4]
    refs = refs[4 + aliased :]
    out_ref = refs.pop(0)
    if is_w:
        wphys_ref = refs.pop(0)
    rhs_ref, res_ref = refs
    width = own_ref.shape[2]
    modes = wphys_ref.shape[1] // 2
    own = own_ref[0]
    even, odd = synthesis([own] + [r[...] for r in far_refs], synth_ref)
    near, away = even + odd, even - odd
    if is_w:
        wphys_ref[:, :modes] = near
        wphys_ref[:, modes:] = away
        near, away = near * near, away * away
    else:
        near, away = near * wphys_ref[:, :modes], away * wphys_ref[:, modes:]
    damp = damp_ref[...]
    for t, term in enumerate(spanwise(near, away, width, [derive_ref])[0]):
        x = own[:, t * LANES : (t + 1) * LANES]
        rhs_ref[t] = x - term - damp * x
    element_solve(rhs_ref, res_ref, inv_ref)
    for t in range(width // LANES):
        out_ref[0, :, t * LANES : (t + 1) * LANES] = res_ref[t]


def whole(shape):
    return pl.BlockSpec(shape, lambda *t: (0,) * len(shape), pipeline_mode=pl.Buffered(1))


def advance(velocity, far, comp, first, rows, wphys, damp, synth, derive, inv, out):
    comps, points, width = velocity.shape
    coefs = 2 * synth.shape[3]
    tiles = width // LANES
    is_w = comp == comps - 1
    at = first // TILE
    row = lambda w: pl.BlockSpec((TILE, w), lambda t: (at + t, 0))
    block = pl.BlockSpec((1, TILE, width), lambda t: (comp, at + t, 0))
    args = [velocity, *far]
    specs = [block] + [pl.BlockSpec((TILE, width), lambda t: (t, 0)) for _ in far]
    if not is_w:
        args.append(wphys)
        specs.append(row(coefs))
    args += [damp, synth, derive, inv]
    specs += [row(LANES), whole(synth.shape), whole(derive.shape), whole(inv.shape)]
    out_shape = [jax.ShapeDtypeStruct(velocity.shape, f32)]
    out_specs = [block]
    aliases = {}
    if out is not None:
        aliases[len(args)] = 0
        args.append(out)
        specs.append(pl.BlockSpec(memory_space=pl.ANY))
    if is_w:
        if wphys is not None:
            aliases[len(args)] = 1
            args.append(wphys)
            specs.append(pl.BlockSpec(memory_space=pl.ANY))
        out_shape.append(jax.ShapeDtypeStruct((points, coefs), f32))
        out_specs.append(row(coefs))
    result = pl.pallas_call(
        lambda *refs: chunk_kernel(len(far), is_w, len(aliases), *refs),
        grid=(rows // TILE,),
        in_specs=specs,
        out_specs=out_specs,
        out_shape=out_shape,
        scratch_shapes=[pltpu.VMEM((tiles, TILE, LANES), f32)] * 2,
        input_output_aliases=aliases,
        compiler_params=pltpu.CompilerParams(vmem_limit_bytes=20 << 20),
        cost_estimate=pl.CostEstimate(
            flops=3 * rows * coefs * (coefs + width), bytes_accessed=8 * rows * width, transcendentals=0
        ),
        name=f"advance_{comp}_{first}",
    )(*args)
    return (result[0], result[1] if is_w else wphys)


def both_kernel(at_ref, own_ref, far_ref, wphys_ref, synth_ref, derive_ref, other_ref, span_ref, *back_refs):
    modes = wphys_ref.shape[1] // 2
    width = far_ref.shape[1]
    even, odd = synthesis([own_ref[0], far_ref[...]], synth_ref)
    near = (even + odd) * wphys_ref[:, :modes]
    away = (even - odd) * wphys_ref[:, modes:]
    here, there = spanwise(near, away, width, [derive_ref, other_ref])
    for t, term in enumerate(here):
        span_ref[:, t * LANES : (t + 1) * LANES] = term
    for ref in back_refs:
        for t in range(0, ref.shape[1], LANES):
            ref[:, t : t + LANES] = there.pop(0)


def both_groups(velocity, comp, at, far, wphys, synth, derive, other, parts):
    width = velocity.shape[2]
    last = far.shape[0] // TILE - 1
    shapes = [(TILE, width)] + [(TILE, LANES * n) for n in parts]
    return pl.pallas_call(
        both_kernel,
        grid_spec=pltpu.PrefetchScalarGridSpec(
            num_scalar_prefetch=1,
            grid=(1,),
            in_specs=[
                pl.BlockSpec((1, TILE, width), lambda t, at: (comp, at[0], 0)),
                pl.BlockSpec((TILE, width), lambda t, at: (last, 0)),
                pl.BlockSpec((TILE, wphys.shape[1]), lambda t, at: (at[0], 0)),
                whole(synth.shape),
                whole(derive.shape),
                whole(other.shape),
            ],
            out_specs=[pl.BlockSpec(shape, lambda t, at: (0, 0)) for shape in shapes],
        ),
        out_shape=[jax.ShapeDtypeStruct(shape, f32) for shape in shapes],
        compiler_params=pltpu.CompilerParams(vmem_limit_bytes=20 << 20),
        name="both_groups",
    )(at, velocity, far, wphys, synth, derive, other)


def finish_kernel(at_ref, own_ref, span_ref, damp_ref, inv_ref, held_ref, out_ref):
    right = []
    for n in range(NODES):
        rows = pl.ds(n, SUB, stride=NODES)
        x = own_ref[0, rows, :]
        right.append(x - span_ref[rows, :] - damp_ref[rows, :] * x)
    for i in range(NODES):
        acc = [None, None]
        for n in range(NODES):
            term = inv_ref[0, i, n : n + 1, :] * right[n]
            acc[n % 2] = term if n < 2 else acc[n % 2] + term
        out_ref[0, pl.ds(i, SUB, stride=NODES), :] = acc[0] + acc[1]


def finish(velocity, comp, at, lane, span, damp, inv, out, name):
    block = pl.BlockSpec((1, TILE, LANES), lambda t, at: (comp, at[0], lane + t))
    return pl.pallas_call(
        finish_kernel,
        grid_spec=pltpu.PrefetchScalarGridSpec(
            num_scalar_prefetch=1,
            grid=(span.shape[1] // LANES,),
            in_specs=[
                block,
                pl.BlockSpec((TILE, LANES), lambda t, at: (0, t)),
                pl.BlockSpec((TILE, LANES), lambda t, at: (at[0], 0)),
                pl.BlockSpec((1, NODES, NODES, LANES), lambda t, at: (lane + t, 0, 0, 0)),
                pl.BlockSpec(memory_space=pl.ANY),
            ],
            out_specs=block,
        ),
        out_shape=jax.ShapeDtypeStruct(velocity.shape, f32),
        input_output_aliases={5: 0},
        compiler_params=pltpu.CompilerParams(vmem_limit_bytes=8 << 20),
        name=name,
    )(at, velocity, span, damp, inv, out)


def exchange(block):
    count = lax.axis_size("mode")
    return [
        lax.ppermute(block, "mode", [(i, (i + s) % count) for i in range(count)])
        for s in range(1, count)
    ]


def sum_over_plane(value):
    count = lax.axis_size("plane")
    if count & (count - 1):
        return lax.psum(value, "plane")
    step = 1
    while step < count:
        value = value + lax.ppermute(value, "plane", [(i, i ^ step) for i in range(count)])
        step *= 2
    return value


def on_device(velocity, inverses, neighbours, flags):
    mode_count = lax.axis_size("mode")
    plane_count = lax.axis_size("plane")
    mine = lax.axis_index("mode")
    comps, points, width = velocity.shape
    coefs = width * mode_count
    elements = neighbours.shape[0]
    w = comps - 1

    first = velocity[w, :TILE]
    far = {(w, 0, TILE): exchange(first)}
    held, velocity = lax.optimization_barrier((first, velocity))
    index = mine * width + lax.iota(jnp.int32, width)
    weight = jnp.where(index < 2, 1.0, 2.0).astype(f32)[None, :]
    blocks = points // TILE
    shared = mode_count == 2 and width > LANES and blocks > 2
    here = jnp.reshape(blocks - 2 + mine, (1,))
    there = jnp.reshape(blocks - 1 - mine if shared else -1, (1,))
    packed, rest = first_pass(velocity, weight, there, shared)
    packed_far = exchange(packed)
    far[w, TILE, points - TILE] = exchange(rest)
    tail, velocity = lax.optimization_barrier((packed, velocity))
    for comp in range(w - 1):
        far[comp, 0, points] = exchange(velocity[comp])
    stop = points - 2 * TILE if shared else points
    for begin in range(0, stop, TILE):
        far[w - 1, begin, TILE] = exchange(velocity[w - 1, begin : begin + TILE])

    packed_far, far[w, 0, TILE] = lax.optimization_barrier((packed_far, far[w, 0, TILE]))
    steps = points // TILE
    parts = jnp.stack([x[:, :, :steps] for x in [packed] + packed_far])
    order = (mine - lax.iota(jnp.int32, mode_count)) % mode_count
    if mode_count == 2:
        sums = parts[0] + parts[1]
    else:
        sums = jnp.sum(jnp.take(parts, order, axis=0), axis=0)
    sums = jnp.transpose(sums, (0, 2, 1)).reshape(2, elements)
    total, high = sums[0], sums[1]
    field = sum_over_plane(jnp.sum(total))
    speed = jnp.sqrt(field / (1.0 * comps * points * plane_count * coefs))
    sensor = jnp.log10((high + 1e-06) / (total + 1e-06))
    ramp = 0.5 * (1.0 + jnp.sin(0.5 * math.pi * jnp.clip(sensor + 2.0, -1.0, 1.0)))
    shape = 0.4 * (1.0 + flags.astype(f32)) * ramp
    forward = [(i, i + 1) for i in range(plane_count - 1)]
    west = lax.ppermute(shape, "plane", forward)
    east = lax.ppermute(shape, "plane", [(b, a) for a, b in forward])
    source = speed * shape
    padded = speed * jnp.concatenate([west, shape, east])
    element = lax.iota(jnp.int32, elements)
    base = jnp.array([0, 2 * elements, elements, elements], dtype=jnp.int32)
    target = jnp.where(neighbours >= 0, base[None, :] + neighbours, elements + element[:, None])
    positions = lax.iota(jnp.int32, 3 * elements)
    picked = jnp.where(target[:, :, None] == positions[None, None, :], padded[None, None, :], 0.0)
    beside = jnp.sum(jnp.sum(picked, axis=2), axis=1)
    viscosity = (2.0 * source + beside) / 6.0
    node = np.arange(NODES)
    degrees = (node // (ORDER + 1)) ** 2 + (node % (ORDER + 1)) ** 2
    factor = (degrees / (2.0 * ORDER * ORDER)).astype(np.float32)
    damp = (viscosity[:, None] * factor[None, :]).reshape(points)
    damp = jnp.broadcast_to(damp[:, None], (points, LANES))

    synth_all, derive_all = (jnp.asarray(x) for x in tables(coefs, width))
    group = lambda table, at: lax.dynamic_index_in_dim(table, at, 0, keepdims=False)
    rows = [group(synth_all, order[s]) for s in range(mode_count)]
    swapped = rows if width > LANES else [rows[s ^ 1] for s in range(mode_count)]
    synth = jnp.stack([jnp.concatenate([x[p] for x in part], axis=1) for p, part in enumerate((rows, swapped))])
    derive = group(derive_all, mine)
    inv = expand(inverses, width)

    out = wphys = back = None
    for (comp, begin, count), blocks in far.items():
        if shared and back is None and comp != w:
            lent = far[w, TILE, points - TILE][0]
            other = group(derive_all, 1 - mine)
            parts = [width // LANES - 1, 1]
            span, *back = both_groups(velocity, w - 1, here, lent, wphys, synth, derive, other, parts)
            back = [exchange(x)[0] for x in back]
            out = finish(velocity, w - 1, here, 0, span, damp, inv, out, "finish_here")
        out, wphys = advance(velocity, blocks, comp, begin, count, wphys, damp, synth, derive, inv, out)
    if shared:
        out = finish(velocity, w - 1, there, 0, back[0], damp, inv, out, "finish_there")
        out = finish(velocity, w - 1, there, parts[0], back[1], damp, inv, out, "finish_last")
    return (out, viscosity)


def solution(mesh):
    in_specs = (P(None, "plane", "mode"), P("mode", None, None), P("plane", None), P("plane"))
    out_specs = (P(None, "plane", "mode"), P("plane"))
    return jax.shard_map(
        on_device, mesh=mesh, in_specs=in_specs, out_specs=out_specs, check_vma=False
    )
```

```python
import math

import jax
import jax.numpy as jnp
import ml_dtypes
import numpy as np
from jax import lax
from jax.experimental import pallas as pl
from jax.experimental.pallas import tpu as pltpu
from jax.sharding import PartitionSpec as P

ORDER = 4
NODES = (ORDER + 1) ** 2
LENGTH = 4.0
LANES = 128
SUB = 8
TILE = SUB * NODES
HEAD = 80

f32 = jnp.float32
bf16 = jnp.bfloat16

IS_HIGH = [n // (ORDER + 1) == ORDER or n % (ORDER + 1) == ORDER for n in range(NODES)]


def split_np(table):
    high = table.astype(np.float32).astype(ml_dtypes.bfloat16)
    low = (table - high.astype(np.float64)).astype(ml_dtypes.bfloat16)
    return np.stack([high, low])


def parity_order(width):
    if width == LANES:
        index = np.arange(width)
        return index[index // 2 % 2 == 0], index[index // 2 % 2 == 1]
    index = np.arange(width).reshape(-1, 2, LANES)
    even = index[:, :, np.arange(LANES) // 2 % 2 == 0]
    odd = index[:, ::-1][:, :, np.arange(LANES) // 2 % 2 == 1]
    return even.reshape(-1), odd.reshape(-1)


def tables(coefs, width):
    modes = coefs // 2
    index = np.arange(coefs)
    pair = index // 2
    odd = index % 2
    freq = np.where(index == 1, modes, pair)
    angle = 2.0 * np.pi * (freq[:, None] * index[None, :modes] % coefs) / coefs
    use_cos = (odd == 0) | (pair == 0)
    basis = np.where(use_cos[:, None], np.cos(angle), -np.sin(angle))
    weight = np.where(pair == 0, 1.0, 2.0)
    rate = pair / (modes * LENGTH * math.sqrt(modes))
    partner = basis[index ^ 1]
    derive = (np.where(odd == 0, -rate, rate) / coefs)[:, None] * partner
    groups = coefs // width
    synth = (weight[:, None] * basis).reshape(groups, width, modes)
    derive = derive.reshape(groups, width, modes).transpose(0, 2, 1)
    orders = parity_order(width)
    synth = np.stack([split_np(synth[:, o]) for o in orders])
    derive = [derive[:, :, o] for o in orders]
    if width == LANES:
        derive = [np.pad(derive[p], ((0, 0), (0, 0), (p * LANES // 2, (1 - p) * LANES // 2))) for p in (0, 1)]
    derive = np.stack([split_np(d) for d in derive])
    return np.moveaxis(synth, 2, 0).copy(), np.moveaxis(derive, 2, 0).copy()


def lane_index(shape):
    return lax.broadcasted_iota(jnp.int32, shape, 1)


def take_lanes(x, index):
    return jnp.take_along_axis(x, index, axis=1, mode="promise_in_bounds")


def deinterleave(first, second):
    lane = lane_index(first.shape)
    half = LANES // 2
    low = lane < half
    place = 4 * (lane % half // 2) + lane % 2
    first = take_lanes(first, place + jnp.where(low, 0, 2))
    second = take_lanes(second, place + jnp.where(low, 2, 0))
    return jnp.where(low, first, second), jnp.where(low, second, first)


def interleave(low_part, high_part, flip):
    lane = lane_index(low_part.shape)
    half = LANES // 2
    both = jnp.where(lane < half, low_part, high_part)
    is_odd = lane // 2 % 2
    upper = 1 - is_odd if flip else is_odd
    return take_lanes(both, lane // 4 * 2 + lane % 2 + upper * half)


def halves(x):
    high = x.astype(bf16)
    return high, (x - high.astype(f32)).astype(bf16)


def dot(a, b):
    return jnp.dot(a, b, preferred_element_type=f32)


def first_kernel(at_ref, vel_ref, weight_ref, energy_ref, rest_ref, point_ref):
    step = pl.program_id(0)
    comps, _, width = vel_ref.shape
    weight = weight_ref[...]
    acc = None
    for lane in range(0, width, LANES):
        for comp in range(comps):
            x = vel_ref[comp, :, lane : lane + LANES]
            term = x * x * weight[:, lane : lane + LANES]
            acc = term if acc is None else acc + term
    point_ref[...] = acc
    total = jnp.zeros((SUB, LANES), f32)
    high = jnp.zeros((SUB, LANES), f32)
    for n in range(NODES):
        part = point_ref[pl.ds(n, SUB, stride=NODES), :]
        total = total + part
        if IS_HIGH[n]:
            high = high + part

    @pl.when(step == 0)
    def _():
        energy_ref[...] = jnp.zeros(energy_ref.shape, f32)

    here = lane_index((SUB, LANES)) == step
    for q, part in enumerate((total, high)):
        energy_ref[q] = jnp.where(here, jnp.sum(part, axis=1, keepdims=True), energy_ref[q])

    @pl.when(step > 0)
    def _():
        rest_ref[pl.ds(pl.multiple_of((step - 1) * TILE, SUB), TILE), :] = vel_ref[comps - 1]

    @pl.when(step == at_ref[0])
    def _():
        rest_ref[rest_ref.shape[0] - TILE :, :] = vel_ref[comps - 2]


def first_pass(velocity, weight, there, lend):
    comps, points, width = velocity.shape
    shape = (2, SUB, LANES)
    rest = points if lend else points - TILE
    return pl.pallas_call(
        first_kernel,
        grid_spec=pltpu.PrefetchScalarGridSpec(
            num_scalar_prefetch=1,
            grid=(points // TILE,),
            in_specs=[
                pl.BlockSpec((comps, TILE, width), lambda t, at: (0, t, 0)),
                pl.BlockSpec((1, width), lambda t, at: (0, 0)),
            ],
            out_specs=[
                pl.BlockSpec(shape, lambda t, at: (0, 0, 0)),
                pl.BlockSpec((rest, width), lambda t, at: (0, 0)),
            ],
            scratch_shapes=[pltpu.VMEM((TILE, LANES), f32)],
        ),
        out_shape=[jax.ShapeDtypeStruct(shape, f32), jax.ShapeDtypeStruct((rest, width), f32)],
        compiler_params=pltpu.CompilerParams(vmem_limit_bytes=16 << 20),
        name="first_pass",
    )(there, velocity, weight)


def expand_kernel(inv_ref, spread_ref, out_ref):
    spread = spread_ref[...]
    for i in range(NODES):
        x = inv_ref[i]
        high, rest = halves(x)
        mid, low = halves(x - high.astype(f32))
        y = (dot(high, spread) + dot(mid, spread)) + dot(low, spread)
        for t in range(out_ref.shape[0]):
            out_ref[t, i] = y[:, t * LANES : (t + 1) * LANES]


def expand(inverses, width):
    pairs = inverses.shape[0]
    spread = np.repeat(np.eye(pairs), 2, axis=1).astype(ml_dtypes.bfloat16)
    return pl.pallas_call(
        expand_kernel,
        out_shape=jax.ShapeDtypeStruct((width // LANES, NODES, NODES, LANES), f32),
        compiler_params=pltpu.CompilerParams(vmem_limit_bytes=16 << 20),
        name="expand",
    )(jnp.transpose(inverses, (1, 2, 0)), spread)


def synthesis(blocks, synth_ref):
    tiles = [x[:, t : t + LANES] for x in blocks for t in range(0, x.shape[1], LANES)]
    pairs = [deinterleave(tiles[t], tiles[t + 1]) for t in range(0, len(tiles), 2)]
    sums = []
    for parity in (0, 1):
        high, low = halves(jnp.concatenate([p[parity] for p in pairs], axis=1))
        first = synth_ref[parity, 0]
        sums.append(dot(high, first) + dot(high, synth_ref[parity, 1]) + dot(low, first))
    return sums


def spanwise(near, away, width, derive_refs):
    parts = [halves(near + away), halves(near - away)]
    groups = []
    for derive_ref in derive_refs:
        span = []
        for parity, (high, low) in enumerate(parts):
            first = derive_ref[parity, 0]
            span.append(dot(high, first) + dot(high, derive_ref[parity, 1]) + dot(low, first))
        if width == LANES:
            groups.append([interleave(span[0], span[1], False)])
            continue
        tiles = []
        for t in range(width // LANES):
            at = slice(t // 2 * LANES, (t // 2 + 1) * LANES)
            tiles.append(interleave(span[t % 2][:, at], span[1 - t % 2][:, at], t % 2 == 1))
        groups.append(tiles)
    return groups


def element_solve(rhs_ref, res_ref, inv_ref):
    def solve(t, carry):
        right = [rhs_ref[t, pl.ds(n, SUB, stride=NODES), :] for n in range(NODES)]
        for i in range(NODES):
            acc = [None, None]
            for n in range(NODES):
                term = inv_ref[t, i, n : n + 1, :] * right[n]
                acc[n % 2] = term if n < 2 else acc[n % 2] + term
            res_ref[t, pl.ds(i, SUB, stride=NODES), :] = acc[0] + acc[1]
        return carry

    lax.fori_loop(0, inv_ref.shape[0], solve, 0)


def chunk_kernel(n_far, is_w, aliased, *refs):
    refs = list(refs)
    own_ref = refs.pop(0)
    far_refs = [refs.pop(0) for _ in range(n_far)]
    wphys_ref = None if is_w else refs.pop(0)
    damp_ref, synth_ref, derive_ref, inv_ref = refs[:4]
    refs = refs[4 + aliased :]
    out_ref = refs.pop(0)
    if is_w:
        wphys_ref = refs.pop(0)
    rhs_ref, res_ref = refs
    width = own_ref.shape[2]
    modes = wphys_ref.shape[1] // 2
    own = own_ref[0]
    even, odd = synthesis([own] + [r[...] for r in far_refs], synth_ref)
    near, away = even + odd, even - odd
    if is_w:
        wphys_ref[:, :modes] = near
        wphys_ref[:, modes:] = away
        near, away = near * near, away * away
    else:
        near, away = near * wphys_ref[:, :modes], away * wphys_ref[:, modes:]
    damp = damp_ref[...]
    for t, term in enumerate(spanwise(near, away, width, [derive_ref])[0]):
        x = own[:, t * LANES : (t + 1) * LANES]
        rhs_ref[t] = x - term - damp * x
    element_solve(rhs_ref, res_ref, inv_ref)
    for t in range(width // LANES):
        out_ref[0, :, t * LANES : (t + 1) * LANES] = res_ref[t]


def whole(shape):
    return pl.BlockSpec(shape, lambda *t: (0,) * len(shape), pipeline_mode=pl.Buffered(1))


def advance(velocity, far, comp, first, rows, wphys, damp, synth, derive, inv, out):
    comps, points, width = velocity.shape
    coefs = 2 * synth.shape[3]
    tiles = width // LANES
    is_w = comp == comps - 1
    at = first // TILE
    row = lambda w: pl.BlockSpec((TILE, w), lambda t: (at + t, 0))
    block = pl.BlockSpec((1, TILE, width), lambda t: (comp, at + t, 0))
    args = [velocity, *far]
    specs = [block] + [pl.BlockSpec((TILE, width), lambda t: (t, 0)) for _ in far]
    if not is_w:
        args.append(wphys)
        specs.append(row(coefs))
    args += [damp, synth, derive, inv]
    specs += [row(LANES), whole(synth.shape), whole(derive.shape), whole(inv.shape)]
    out_shape = [jax.ShapeDtypeStruct(velocity.shape, f32)]
    out_specs = [block]
    aliases = {}
    if out is not None:
        aliases[len(args)] = 0
        args.append(out)
        specs.append(pl.BlockSpec(memory_space=pl.ANY))
    if is_w:
        if wphys is not None:
            aliases[len(args)] = 1
            args.append(wphys)
            specs.append(pl.BlockSpec(memory_space=pl.ANY))
        out_shape.append(jax.ShapeDtypeStruct((points, coefs), f32))
        out_specs.append(row(coefs))
    result = pl.pallas_call(
        lambda *refs: chunk_kernel(len(far), is_w, len(aliases), *refs),
        grid=(rows // TILE,),
        in_specs=specs,
        out_specs=out_specs,
        out_shape=out_shape,
        scratch_shapes=[pltpu.VMEM((tiles, TILE, LANES), f32)] * 2,
        input_output_aliases=aliases,
        compiler_params=pltpu.CompilerParams(vmem_limit_bytes=20 << 20),
        cost_estimate=pl.CostEstimate(
            flops=3 * rows * coefs * (coefs + width), bytes_accessed=8 * rows * width, transcendentals=0
        ),
        name=f"advance_{comp}_{first}",
    )(*args)
    return (result[0], result[1] if is_w else wphys)


def both_kernel(at_ref, own_ref, far_ref, wphys_ref, synth_ref, derive_ref, other_ref, span_ref, *back_refs):
    modes = wphys_ref.shape[1] // 2
    width = far_ref.shape[1]
    even, odd = synthesis([own_ref[0], far_ref[...]], synth_ref)
    near = (even + odd) * wphys_ref[:, :modes]
    away = (even - odd) * wphys_ref[:, modes:]
    here, there = spanwise(near, away, width, [derive_ref, other_ref])
    for t, term in enumerate(here):
        span_ref[:, t * LANES : (t + 1) * LANES] = term
    for ref in back_refs:
        for t in range(0, ref.shape[1], LANES):
            ref[:, t : t + LANES] = there.pop(0)


def both_groups(velocity, comp, at, far, wphys, synth, derive, other, parts):
    width = velocity.shape[2]
    last = far.shape[0] // TILE - 1
    shapes = [(TILE, width)] + [(TILE, LANES * n) for n in parts]
    return pl.pallas_call(
        both_kernel,
        grid_spec=pltpu.PrefetchScalarGridSpec(
            num_scalar_prefetch=1,
            grid=(1,),
            in_specs=[
                pl.BlockSpec((1, TILE, width), lambda t, at: (comp, at[0], 0)),
                pl.BlockSpec((TILE, width), lambda t, at: (last, 0)),
                pl.BlockSpec((TILE, wphys.shape[1]), lambda t, at: (at[0], 0)),
                whole(synth.shape),
                whole(derive.shape),
                whole(other.shape),
            ],
            out_specs=[pl.BlockSpec(shape, lambda t, at: (0, 0)) for shape in shapes],
        ),
        out_shape=[jax.ShapeDtypeStruct(shape, f32) for shape in shapes],
        compiler_params=pltpu.CompilerParams(vmem_limit_bytes=20 << 20),
        name="both_groups",
    )(at, velocity, far, wphys, synth, derive, other)


def finish_kernel(at_ref, own_ref, span_ref, damp_ref, inv_ref, held_ref, out_ref):
    right = []
    for n in range(NODES):
        rows = pl.ds(n, SUB, stride=NODES)
        x = own_ref[0, rows, :]
        right.append(x - span_ref[rows, :] - damp_ref[rows, :] * x)
    for i in range(NODES):
        acc = [None, None]
        for n in range(NODES):
            term = inv_ref[0, i, n : n + 1, :] * right[n]
            acc[n % 2] = term if n < 2 else acc[n % 2] + term
        out_ref[0, pl.ds(i, SUB, stride=NODES), :] = acc[0] + acc[1]


def finish(velocity, comp, at, lane, span, damp, inv, out, name):
    block = pl.BlockSpec((1, TILE, LANES), lambda t, at: (comp, at[0], lane + t))
    return pl.pallas_call(
        finish_kernel,
        grid_spec=pltpu.PrefetchScalarGridSpec(
            num_scalar_prefetch=1,
            grid=(span.shape[1] // LANES,),
            in_specs=[
                block,
                pl.BlockSpec((TILE, LANES), lambda t, at: (0, t)),
                pl.BlockSpec((TILE, LANES), lambda t, at: (at[0], 0)),
                pl.BlockSpec((1, NODES, NODES, LANES), lambda t, at: (lane + t, 0, 0, 0)),
                pl.BlockSpec(memory_space=pl.ANY),
            ],
            out_specs=block,
        ),
        out_shape=jax.ShapeDtypeStruct(velocity.shape, f32),
        input_output_aliases={5: 0},
        compiler_params=pltpu.CompilerParams(vmem_limit_bytes=8 << 20),
        name=name,
    )(at, velocity, span, damp, inv, out)


def exchange(block):
    count = lax.axis_size("mode")
    return [
        lax.ppermute(block, "mode", [(i, (i + s) % count) for i in range(count)])
        for s in range(1, count)
    ]


def sum_over_plane(value):
    count = lax.axis_size("plane")
    if count & (count - 1):
        return lax.psum(value, "plane")
    step = 1
    while step < count:
        value = value + lax.ppermute(value, "plane", [(i, i ^ step) for i in range(count)])
        step *= 2
    return value


def on_device(velocity, inverses, neighbours, flags):
    mode_count = lax.axis_size("mode")
    plane_count = lax.axis_size("plane")
    mine = lax.axis_index("mode")
    comps, points, width = velocity.shape
    coefs = width * mode_count
    elements = neighbours.shape[0]
    w = comps - 1

    pieces = []
    for begin, end in ((0, HEAD), (HEAD, TILE)):
        first = velocity[w, begin:end]
        pieces.append(exchange(first))
        held, velocity = lax.optimization_barrier((first, velocity))
    far = {(w, 0, TILE): [jnp.concatenate(x) for x in zip(*pieces)]}
    index = mine * width + lax.iota(jnp.int32, width)
    weight = jnp.where(index < 2, 1.0, 2.0).astype(f32)[None, :]
    blocks = points // TILE
    shared = mode_count == 2 and width > LANES and blocks > 2
    here = jnp.reshape(blocks - 2 + mine, (1,))
    there = jnp.reshape(blocks - 1 - mine if shared else -1, (1,))
    packed, rest = first_pass(velocity, weight, there, shared)
    packed_far = exchange(packed)
    far[w, TILE, points - TILE] = exchange(rest)
    tail, velocity = lax.optimization_barrier((packed, velocity))
    for comp in range(w - 1):
        far[comp, 0, points] = exchange(velocity[comp])
    stop = points - 2 * TILE if shared else points
    for begin in range(0, stop, TILE):
        far[w - 1, begin, TILE] = exchange(velocity[w - 1, begin : begin + TILE])

    packed_far, far[w, 0, TILE] = lax.optimization_barrier((packed_far, far[w, 0, TILE]))
    steps = points // TILE
    parts = jnp.stack([x[:, :, :steps] for x in [packed] + packed_far])
    order = (mine - lax.iota(jnp.int32, mode_count)) % mode_count
    if mode_count == 2:
        sums = parts[0] + parts[1]
    else:
        sums = jnp.sum(jnp.take(parts, order, axis=0), axis=0)
    sums = jnp.transpose(sums, (0, 2, 1)).reshape(2, elements)
    total, high = sums[0], sums[1]
    field = sum_over_plane(jnp.sum(total))
    speed = jnp.sqrt(field / (1.0 * comps * points * plane_count * coefs))
    sensor = jnp.log10((high + 1e-06) / (total + 1e-06))
    ramp = 0.5 * (1.0 + jnp.sin(0.5 * math.pi * jnp.clip(sensor + 2.0, -1.0, 1.0)))
    shape = 0.4 * (1.0 + flags.astype(f32)) * ramp
    forward = [(i, i + 1) for i in range(plane_count - 1)]
    west = lax.ppermute(shape, "plane", forward)
    east = lax.ppermute(shape, "plane", [(b, a) for a, b in forward])
    source = speed * shape
    padded = speed * jnp.concatenate([west, shape, east])
    element = lax.iota(jnp.int32, elements)
    base = jnp.array([0, 2 * elements, elements, elements], dtype=jnp.int32)
    target = jnp.where(neighbours >= 0, base[None, :] + neighbours, elements + element[:, None])
    positions = lax.iota(jnp.int32, 3 * elements)
    picked = jnp.where(target[:, :, None] == positions[None, None, :], padded[None, None, :], 0.0)
    beside = jnp.sum(jnp.sum(picked, axis=2), axis=1)
    viscosity = (2.0 * source + beside) / 6.0
    node = np.arange(NODES)
    degrees = (node // (ORDER + 1)) ** 2 + (node % (ORDER + 1)) ** 2
    factor = (degrees / (2.0 * ORDER * ORDER)).astype(np.float32)
    damp = (viscosity[:, None] * factor[None, :]).reshape(points)
    damp = jnp.broadcast_to(damp[:, None], (points, LANES))

    synth_all, derive_all = (jnp.asarray(x) for x in tables(coefs, width))
    group = lambda table, at: lax.dynamic_index_in_dim(table, at, 0, keepdims=False)
    rows = [group(synth_all, order[s]) for s in range(mode_count)]
    swapped = rows if width > LANES else [rows[s ^ 1] for s in range(mode_count)]
    synth = jnp.stack([jnp.concatenate([x[p] for x in part], axis=1) for p, part in enumerate((rows, swapped))])
    derive = group(derive_all, mine)
    inv = expand(inverses, width)

    out = wphys = back = None
    for (comp, begin, count), blocks in far.items():
        if shared and back is None and comp != w:
            lent = far[w, TILE, points - TILE][0]
            other = group(derive_all, 1 - mine)
            parts = [width // LANES - 2, 1, 1] if width > 2 * LANES else [1, 1]
            span, *back = both_groups(velocity, w - 1, here, lent, wphys, synth, derive, other, parts)
            back = [exchange(x)[0] for x in back]
            out = finish(velocity, w - 1, here, 0, span, damp, inv, out, "finish_here")
        out, wphys = advance(velocity, blocks, comp, begin, count, wphys, damp, synth, derive, inv, out)
    if shared:
        lane = 0
        for term, count in zip(back, parts):
            out = finish(velocity, w - 1, there, lane, term, damp, inv, out, f"finish_there_{lane}")
            lane += count
    return (out, viscosity)


def solution(mesh):
    in_specs = (P(None, "plane", "mode"), P("mode", None, None), P("plane", None), P("plane"))
    out_specs = (P(None, "plane", "mode"), P("plane"))
    return jax.shard_map(
        on_device, mesh=mesh, in_specs=in_specs, out_specs=out_specs, check_vma=False
    )
```

```python
import math

import jax
import jax.numpy as jnp
import ml_dtypes
import numpy as np
from jax import lax
from jax.experimental import pallas as pl
from jax.experimental.pallas import tpu as pltpu
from jax.sharding import PartitionSpec as P

ORDER = 4
NODES = (ORDER + 1) ** 2
LENGTH = 4.0
LANES = 128
SUB = 8
TILE = SUB * NODES
HEAD = 80

f32 = jnp.float32
bf16 = jnp.bfloat16

IS_HIGH = [n // (ORDER + 1) == ORDER or n % (ORDER + 1) == ORDER for n in range(NODES)]


def split_np(table):
    high = table.astype(np.float32).astype(ml_dtypes.bfloat16)
    low = (table - high.astype(np.float64)).astype(ml_dtypes.bfloat16)
    return np.stack([high, low])


def parity_order(width):
    if width == LANES:
        index = np.arange(width)
        return index[index // 2 % 2 == 0], index[index // 2 % 2 == 1]
    index = np.arange(width).reshape(-1, 2, LANES)
    even = index[:, :, np.arange(LANES) // 2 % 2 == 0]
    odd = index[:, ::-1][:, :, np.arange(LANES) // 2 % 2 == 1]
    return even.reshape(-1), odd.reshape(-1)


def tables(coefs, width):
    modes = coefs // 2
    index = np.arange(coefs)
    pair = index // 2
    odd = index % 2
    freq = np.where(index == 1, modes, pair)
    angle = 2.0 * np.pi * (freq[:, None] * index[None, :modes] % coefs) / coefs
    use_cos = (odd == 0) | (pair == 0)
    basis = np.where(use_cos[:, None], np.cos(angle), -np.sin(angle))
    weight = np.where(pair == 0, 1.0, 2.0)
    rate = pair / (modes * LENGTH * math.sqrt(modes))
    partner = basis[index ^ 1]
    derive = (np.where(odd == 0, -rate, rate) / coefs)[:, None] * partner
    groups = coefs // width
    synth = (weight[:, None] * basis).reshape(groups, width, modes)
    derive = derive.reshape(groups, width, modes).transpose(0, 2, 1)
    orders = parity_order(width)
    synth = np.stack([split_np(synth[:, o]) for o in orders])
    derive = [derive[:, :, o] for o in orders]
    if width == LANES:
        derive = [np.pad(derive[p], ((0, 0), (0, 0), (p * LANES // 2, (1 - p) * LANES // 2))) for p in (0, 1)]
    derive = np.stack([split_np(d) for d in derive])
    return np.moveaxis(synth, 2, 0).copy(), np.moveaxis(derive, 2, 0).copy()


def lane_index(shape):
    return lax.broadcasted_iota(jnp.int32, shape, 1)


def take_lanes(x, index):
    return jnp.take_along_axis(x, index, axis=1, mode="promise_in_bounds")


def deinterleave(first, second):
    lane = lane_index(first.shape)
    half = LANES // 2
    low = lane < half
    place = 4 * (lane % half // 2) + lane % 2
    first = take_lanes(first, place + jnp.where(low, 0, 2))
    second = take_lanes(second, place + jnp.where(low, 2, 0))
    return jnp.where(low, first, second), jnp.where(low, second, first)


def interleave(low_part, high_part, flip):
    lane = lane_index(low_part.shape)
    half = LANES // 2
    both = jnp.where(lane < half, low_part, high_part)
    is_odd = lane // 2 % 2
    upper = 1 - is_odd if flip else is_odd
    return take_lanes(both, lane // 4 * 2 + lane % 2 + upper * half)


def halves(x):
    high = x.astype(bf16)
    return high, (x - high.astype(f32)).astype(bf16)


def dot(a, b):
    return jnp.dot(a, b, preferred_element_type=f32)


def first_kernel(at_ref, vel_ref, weight_ref, energy_ref, rest_ref, point_ref):
    step = pl.program_id(0)
    comps, _, width = vel_ref.shape
    weight = weight_ref[...]
    acc = None
    for lane in range(0, width, LANES):
        for comp in range(comps):
            x = vel_ref[comp, :, lane : lane + LANES]
            term = x * x * weight[:, lane : lane + LANES]
            acc = term if acc is None else acc + term
    point_ref[...] = acc
    total = jnp.zeros((SUB, LANES), f32)
    high = jnp.zeros((SUB, LANES), f32)
    for n in range(NODES):
        part = point_ref[pl.ds(n, SUB, stride=NODES), :]
        total = total + part
        if IS_HIGH[n]:
            high = high + part

    @pl.when(step == 0)
    def _():
        energy_ref[...] = jnp.zeros(energy_ref.shape, f32)

    here = lane_index((SUB, LANES)) == step
    for q, part in enumerate((total, high)):
        energy_ref[q] = jnp.where(here, jnp.sum(part, axis=1, keepdims=True), energy_ref[q])

    @pl.when(step > 0)
    def _():
        rest_ref[pl.ds(pl.multiple_of((step - 1) * TILE, SUB), TILE), :] = vel_ref[comps - 1]

    @pl.when(step == at_ref[0])
    def _():
        rest_ref[rest_ref.shape[0] - TILE :, :] = vel_ref[comps - 2]


def first_pass(velocity, weight, there, lend):
    comps, points, width = velocity.shape
    shape = (2, SUB, LANES)
    rest = points if lend else points - TILE
    return pl.pallas_call(
        first_kernel,
        grid_spec=pltpu.PrefetchScalarGridSpec(
            num_scalar_prefetch=1,
            grid=(points // TILE,),
            in_specs=[
                pl.BlockSpec((comps, TILE, width), lambda t, at: (0, t, 0)),
                pl.BlockSpec((1, width), lambda t, at: (0, 0)),
            ],
            out_specs=[
                pl.BlockSpec(shape, lambda t, at: (0, 0, 0)),
                pl.BlockSpec((rest, width), lambda t, at: (0, 0)),
            ],
            scratch_shapes=[pltpu.VMEM((TILE, LANES), f32)],
        ),
        out_shape=[jax.ShapeDtypeStruct(shape, f32), jax.ShapeDtypeStruct((rest, width), f32)],
        compiler_params=pltpu.CompilerParams(vmem_limit_bytes=16 << 20),
        name="first_pass",
    )(there, velocity, weight)


def expand_kernel(inv_ref, spread_ref, out_ref):
    spread = spread_ref[...]
    for i in range(NODES):
        x = inv_ref[i]
        high, rest = halves(x)
        mid, low = halves(x - high.astype(f32))
        y = (dot(high, spread) + dot(mid, spread)) + dot(low, spread)
        for t in range(out_ref.shape[0]):
            out_ref[t, i] = y[:, t * LANES : (t + 1) * LANES]


def expand(inverses, width):
    pairs = inverses.shape[0]
    spread = np.repeat(np.eye(pairs), 2, axis=1).astype(ml_dtypes.bfloat16)
    return pl.pallas_call(
        expand_kernel,
        out_shape=jax.ShapeDtypeStruct((width // LANES, NODES, NODES, LANES), f32),
        compiler_params=pltpu.CompilerParams(vmem_limit_bytes=16 << 20),
        name="expand",
    )(jnp.transpose(inverses, (1, 2, 0)), spread)


def synthesis(blocks, synth_ref):
    tiles = [x[:, t : t + LANES] for x in blocks for t in range(0, x.shape[1], LANES)]
    pairs = [deinterleave(tiles[t], tiles[t + 1]) for t in range(0, len(tiles), 2)]
    sums = []
    for parity in (0, 1):
        high, low = halves(jnp.concatenate([p[parity] for p in pairs], axis=1))
        first = synth_ref[parity, 0]
        sums.append(dot(high, first) + dot(high, synth_ref[parity, 1]) + dot(low, first))
    return sums


def spanwise(near, away, width, derive_refs):
    parts = [halves(near + away), halves(near - away)]
    groups = []
    for derive_ref in derive_refs:
        span = []
        for parity, (high, low) in enumerate(parts):
            first = derive_ref[parity, 0]
            span.append(dot(high, first) + dot(high, derive_ref[parity, 1]) + dot(low, first))
        if width == LANES:
            groups.append([interleave(span[0], span[1], False)])
            continue
        tiles = []
        for t in range(width // LANES):
            at = slice(t // 2 * LANES, (t // 2 + 1) * LANES)
            tiles.append(interleave(span[t % 2][:, at], span[1 - t % 2][:, at], t % 2 == 1))
        groups.append(tiles)
    return groups


def element_solve(rhs_ref, res_ref, inv_ref):
    def solve(t, carry):
        right = [rhs_ref[t, pl.ds(n, SUB, stride=NODES), :] for n in range(NODES)]
        for i in range(NODES):
            acc = [None, None]
            for n in range(NODES):
                term = inv_ref[t, i, n : n + 1, :] * right[n]
                acc[n % 2] = term if n < 2 else acc[n % 2] + term
            res_ref[t, pl.ds(i, SUB, stride=NODES), :] = acc[0] + acc[1]
        return carry

    lax.fori_loop(0, inv_ref.shape[0], solve, 0)


def chunk_kernel(n_far, is_w, aliased, *refs):
    refs = list(refs)
    own_ref = refs.pop(0)
    far_refs = [refs.pop(0) for _ in range(n_far)]
    wphys_ref = None if is_w else refs.pop(0)
    damp_ref, synth_ref, derive_ref, inv_ref = refs[:4]
    refs = refs[4 + aliased :]
    out_ref = refs.pop(0)
    if is_w:
        wphys_ref = refs.pop(0)
    rhs_ref, res_ref = refs
    width = own_ref.shape[2]
    modes = wphys_ref.shape[1] // 2
    own = own_ref[0]
    even, odd = synthesis([own] + [r[...] for r in far_refs], synth_ref)
    near, away = even + odd, even - odd
    if is_w:
        wphys_ref[:, :modes] = near
        wphys_ref[:, modes:] = away
        near, away = near * near, away * away
    else:
        near, away = near * wphys_ref[:, :modes], away * wphys_ref[:, modes:]
    damp = damp_ref[...]
    for t, term in enumerate(spanwise(near, away, width, [derive_ref])[0]):
        x = own[:, t * LANES : (t + 1) * LANES]
        rhs_ref[t] = x - term - damp * x
    element_solve(rhs_ref, res_ref, inv_ref)
    for t in range(width // LANES):
        out_ref[0, :, t * LANES : (t + 1) * LANES] = res_ref[t]


def whole(shape):
    return pl.BlockSpec(shape, lambda *t: (0,) * len(shape), pipeline_mode=pl.Buffered(1))


def advance(velocity, far, comp, first, rows, wphys, damp, synth, derive, inv, out):
    comps, points, width = velocity.shape
    coefs = 2 * synth.shape[3]
    tiles = width // LANES
    is_w = comp == comps - 1
    at = first // TILE
    row = lambda w: pl.BlockSpec((TILE, w), lambda t: (at + t, 0))
    block = pl.BlockSpec((1, TILE, width), lambda t: (comp, at + t, 0))
    args = [velocity, *far]
    specs = [block] + [pl.BlockSpec((TILE, width), lambda t: (t, 0)) for _ in far]
    if not is_w:
        args.append(wphys)
        specs.append(row(coefs))
    args += [damp, synth, derive, inv]
    specs += [row(LANES), whole(synth.shape), whole(derive.shape), whole(inv.shape)]
    out_shape = [jax.ShapeDtypeStruct(velocity.shape, f32)]
    out_specs = [block]
    aliases = {}
    if out is not None:
        aliases[len(args)] = 0
        args.append(out)
        specs.append(pl.BlockSpec(memory_space=pl.ANY))
    if is_w:
        if wphys is not None:
            aliases[len(args)] = 1
            args.append(wphys)
            specs.append(pl.BlockSpec(memory_space=pl.ANY))
        out_shape.append(jax.ShapeDtypeStruct((points, coefs), f32))
        out_specs.append(row(coefs))
    result = pl.pallas_call(
        lambda *refs: chunk_kernel(len(far), is_w, len(aliases), *refs),
        grid=(rows // TILE,),
        in_specs=specs,
        out_specs=out_specs,
        out_shape=out_shape,
        scratch_shapes=[pltpu.VMEM((tiles, TILE, LANES), f32)] * 2,
        input_output_aliases=aliases,
        compiler_params=pltpu.CompilerParams(vmem_limit_bytes=20 << 20),
        cost_estimate=pl.CostEstimate(
            flops=3 * rows * coefs * (coefs + width), bytes_accessed=8 * rows * width, transcendentals=0
        ),
        name=f"advance_{comp}_{first}",
    )(*args)
    return (result[0], result[1] if is_w else wphys)


def both_kernel(at_ref, own_ref, far_ref, wphys_ref, synth_ref, derive_ref, other_ref, span_ref, *back_refs):
    modes = wphys_ref.shape[1] // 2
    width = far_ref.shape[1]
    even, odd = synthesis([own_ref[0], far_ref[...]], synth_ref)
    near = (even + odd) * wphys_ref[:, :modes]
    away = (even - odd) * wphys_ref[:, modes:]
    here, there = spanwise(near, away, width, [derive_ref, other_ref])
    for t, term in enumerate(here):
        span_ref[:, t * LANES : (t + 1) * LANES] = term
    for ref in back_refs:
        for t in range(0, ref.shape[1], LANES):
            ref[:, t : t + LANES] = there.pop(0)


def both_groups(velocity, comp, at, far, wphys, synth, derive, other, parts):
    width = velocity.shape[2]
    last = far.shape[0] // TILE - 1
    shapes = [(TILE, width)] + [(TILE, LANES * n) for n in parts]
    return pl.pallas_call(
        both_kernel,
        grid_spec=pltpu.PrefetchScalarGridSpec(
            num_scalar_prefetch=1,
            grid=(1,),
            in_specs=[
                pl.BlockSpec((1, TILE, width), lambda t, at: (comp, at[0], 0)),
                pl.BlockSpec((TILE, width), lambda t, at: (last, 0)),
                pl.BlockSpec((TILE, wphys.shape[1]), lambda t, at: (at[0], 0)),
                whole(synth.shape),
                whole(derive.shape),
                whole(other.shape),
            ],
            out_specs=[pl.BlockSpec(shape, lambda t, at: (0, 0)) for shape in shapes],
        ),
        out_shape=[jax.ShapeDtypeStruct(shape, f32) for shape in shapes],
        compiler_params=pltpu.CompilerParams(vmem_limit_bytes=20 << 20),
        name="both_groups",
    )(at, velocity, far, wphys, synth, derive, other)


def finish_kernel(at_ref, own_ref, span_ref, damp_ref, inv_ref, held_ref, out_ref):
    right = []
    for n in range(NODES):
        rows = pl.ds(n, SUB, stride=NODES)
        x = own_ref[0, rows, :]
        right.append(x - span_ref[rows, :] - damp_ref[rows, :] * x)
    for i in range(NODES):
        acc = [None, None]
        for n in range(NODES):
            term = inv_ref[0, i, n : n + 1, :] * right[n]
            acc[n % 2] = term if n < 2 else acc[n % 2] + term
        out_ref[0, pl.ds(i, SUB, stride=NODES), :] = acc[0] + acc[1]


def finish(velocity, comp, at, lane, span, damp, inv, out, name):
    block = pl.BlockSpec((1, TILE, LANES), lambda t, at: (comp, at[0], lane + t))
    return pl.pallas_call(
        finish_kernel,
        grid_spec=pltpu.PrefetchScalarGridSpec(
            num_scalar_prefetch=1,
            grid=(span.shape[1] // LANES,),
            in_specs=[
                block,
                pl.BlockSpec((TILE, LANES), lambda t, at: (0, t)),
                pl.BlockSpec((TILE, LANES), lambda t, at: (at[0], 0)),
                pl.BlockSpec((1, NODES, NODES, LANES), lambda t, at: (lane + t, 0, 0, 0)),
                pl.BlockSpec(memory_space=pl.ANY),
            ],
            out_specs=block,
        ),
        out_shape=jax.ShapeDtypeStruct(velocity.shape, f32),
        input_output_aliases={5: 0},
        compiler_params=pltpu.CompilerParams(vmem_limit_bytes=8 << 20),
        name=name,
    )(at, velocity, span, damp, inv, out)


def exchange(block):
    count = lax.axis_size("mode")
    return [
        lax.ppermute(block, "mode", [(i, (i + s) % count) for i in range(count)])
        for s in range(1, count)
    ]


def sum_over_plane(value):
    count = lax.axis_size("plane")
    if count & (count - 1):
        return lax.psum(value, "plane")
    step = 1
    while step < count:
        value = value + lax.ppermute(value, "plane", [(i, i ^ step) for i in range(count)])
        step *= 2
    return value


def on_device(velocity, inverses, neighbours, flags):
    mode_count = lax.axis_size("mode")
    plane_count = lax.axis_size("plane")
    mine = lax.axis_index("mode")
    comps, points, width = velocity.shape
    coefs = width * mode_count
    elements = neighbours.shape[0]
    w = comps - 1

    pieces = []
    for begin, end in ((0, HEAD), (HEAD, TILE)):
        first = velocity[w, begin:end]
        pieces.append(exchange(first))
        held, velocity = lax.optimization_barrier((first, velocity))
    far = {(w, 0, TILE): [jnp.concatenate(x) for x in zip(*pieces)]}
    index = mine * width + lax.iota(jnp.int32, width)
    weight = jnp.where(index < 2, 1.0, 2.0).astype(f32)[None, :]
    blocks = points // TILE
    shared = mode_count == 2 and width > LANES and blocks > 2
    here = jnp.reshape(blocks - 2 + mine, (1,))
    there = jnp.reshape(blocks - 1 - mine if shared else -1, (1,))
    packed, rest = first_pass(velocity, weight, there, shared)
    packed_far = exchange(packed)
    far[w, TILE, points - TILE] = exchange(rest)
    tail, velocity = lax.optimization_barrier((packed, velocity))
    for comp in range(w - 1):
        for begin, end in ((0, points - TILE), (points - TILE, points)):
            far[comp, begin, end - begin] = exchange(velocity[comp, begin:end])
    stop = points - 2 * TILE if shared else points
    for begin in range(0, stop, TILE):
        far[w - 1, begin, TILE] = exchange(velocity[w - 1, begin : begin + TILE])

    packed_far, far[w, 0, TILE] = lax.optimization_barrier((packed_far, far[w, 0, TILE]))
    steps = points // TILE
    parts = jnp.stack([x[:, :, :steps] for x in [packed] + packed_far])
    order = (mine - lax.iota(jnp.int32, mode_count)) % mode_count
    if mode_count == 2:
        sums = parts[0] + parts[1]
    else:
        sums = jnp.sum(jnp.take(parts, order, axis=0), axis=0)
    sums = jnp.transpose(sums, (0, 2, 1)).reshape(2, elements)
    total, high = sums[0], sums[1]
    field = sum_over_plane(jnp.sum(total))
    speed = jnp.sqrt(field / (1.0 * comps * points * plane_count * coefs))
    sensor = jnp.log10((high + 1e-06) / (total + 1e-06))
    ramp = 0.5 * (1.0 + jnp.sin(0.5 * math.pi * jnp.clip(sensor + 2.0, -1.0, 1.0)))
    shape = 0.4 * (1.0 + flags.astype(f32)) * ramp
    forward = [(i, i + 1) for i in range(plane_count - 1)]
    west = lax.ppermute(shape, "plane", forward)
    east = lax.ppermute(shape, "plane", [(b, a) for a, b in forward])
    source = speed * shape
    padded = speed * jnp.concatenate([west, shape, east])
    element = lax.iota(jnp.int32, elements)
    base = jnp.array([0, 2 * elements, elements, elements], dtype=jnp.int32)
    target = jnp.where(neighbours >= 0, base[None, :] + neighbours, elements + element[:, None])
    positions = lax.iota(jnp.int32, 3 * elements)
    picked = jnp.where(target[:, :, None] == positions[None, None, :], padded[None, None, :], 0.0)
    beside = jnp.sum(jnp.sum(picked, axis=2), axis=1)
    viscosity = (2.0 * source + beside) / 6.0
    node = np.arange(NODES)
    degrees = (node // (ORDER + 1)) ** 2 + (node % (ORDER + 1)) ** 2
    factor = (degrees / (2.0 * ORDER * ORDER)).astype(np.float32)
    damp = (viscosity[:, None] * factor[None, :]).reshape(points)
    damp = jnp.broadcast_to(damp[:, None], (points, LANES))

    synth_all, derive_all = (jnp.asarray(x) for x in tables(coefs, width))
    group = lambda table, at: lax.dynamic_index_in_dim(table, at, 0, keepdims=False)
    rows = [group(synth_all, order[s]) for s in range(mode_count)]
    swapped = rows if width > LANES else [rows[s ^ 1] for s in range(mode_count)]
    synth = jnp.stack([jnp.concatenate([x[p] for x in part], axis=1) for p, part in enumerate((rows, swapped))])
    derive = group(derive_all, mine)
    inv = expand(inverses, width)

    out = wphys = back = None
    for (comp, begin, count), blocks in far.items():
        if shared and back is None and comp != w:
            lent = far[w, TILE, points - TILE][0]
            other = group(derive_all, 1 - mine)
            parts = [width // LANES - 2, 1, 1] if width > 2 * LANES else [1, 1]
            span, *back = both_groups(velocity, w - 1, here, lent, wphys, synth, derive, other, parts)
            back = [exchange(x)[0] for x in back]
            out = finish(velocity, w - 1, here, 0, span, damp, inv, out, "finish_here")
        out, wphys = advance(velocity, blocks, comp, begin, count, wphys, damp, synth, derive, inv, out)
    if shared:
        lane = 0
        for term, count in zip(back, parts):
            out = finish(velocity, w - 1, there, lane, term, damp, inv, out, f"finish_there_{lane}")
            lane += count
    return (out, viscosity)


def solution(mesh):
    in_specs = (P(None, "plane", "mode"), P("mode", None, None), P("plane", None), P("plane"))
    out_specs = (P(None, "plane", "mode"), P("plane"))
    return jax.shard_map(
        on_device, mesh=mesh, in_specs=in_specs, out_specs=out_specs, check_vma=False
    )
```

```python
import math

import jax
import jax.numpy as jnp
import ml_dtypes
import numpy as np
from jax import lax
from jax.experimental import pallas as pl
from jax.experimental.pallas import tpu as pltpu
from jax.sharding import PartitionSpec as P

ORDER = 4
NODES = (ORDER + 1) ** 2
LENGTH = 4.0
LANES = 128
SUB = 8
TILE = SUB * NODES
HEAD = 80

f32 = jnp.float32
bf16 = jnp.bfloat16

IS_HIGH = [n // (ORDER + 1) == ORDER or n % (ORDER + 1) == ORDER for n in range(NODES)]


def split_np(table):
    high = table.astype(np.float32).astype(ml_dtypes.bfloat16)
    low = (table - high.astype(np.float64)).astype(ml_dtypes.bfloat16)
    return np.stack([high, low])


def parity_order(width):
    if width == LANES:
        index = np.arange(width)
        return index[index // 2 % 2 == 0], index[index // 2 % 2 == 1]
    index = np.arange(width).reshape(-1, 2, LANES)
    even = index[:, :, np.arange(LANES) // 2 % 2 == 0]
    odd = index[:, ::-1][:, :, np.arange(LANES) // 2 % 2 == 1]
    return even.reshape(-1), odd.reshape(-1)


def tables(coefs, width):
    modes = coefs // 2
    index = np.arange(coefs)
    pair = index // 2
    odd = index % 2
    freq = np.where(index == 1, modes, pair)
    angle = 2.0 * np.pi * (freq[:, None] * index[None, :modes] % coefs) / coefs
    use_cos = (odd == 0) | (pair == 0)
    basis = np.where(use_cos[:, None], np.cos(angle), -np.sin(angle))
    weight = np.where(pair == 0, 1.0, 2.0)
    rate = pair / (modes * LENGTH * math.sqrt(modes))
    partner = basis[index ^ 1]
    derive = (np.where(odd == 0, -rate, rate) / coefs)[:, None] * partner
    groups = coefs // width
    synth = (weight[:, None] * basis).reshape(groups, width, modes)
    derive = derive.reshape(groups, width, modes).transpose(0, 2, 1)
    orders = parity_order(width)
    synth = np.stack([split_np(synth[:, o]) for o in orders])
    derive = [derive[:, :, o] for o in orders]
    if width == LANES:
        derive = [np.pad(derive[p], ((0, 0), (0, 0), (p * LANES // 2, (1 - p) * LANES // 2))) for p in (0, 1)]
    derive = np.stack([split_np(d) for d in derive])
    return np.moveaxis(synth, 2, 0).copy(), np.moveaxis(derive, 2, 0).copy()


def lane_index(shape):
    return lax.broadcasted_iota(jnp.int32, shape, 1)


def take_lanes(x, index):
    return jnp.take_along_axis(x, index, axis=1, mode="promise_in_bounds")


def deinterleave(first, second):
    lane = lane_index(first.shape)
    half = LANES // 2
    low = lane < half
    place = 4 * (lane % half // 2) + lane % 2
    first = take_lanes(first, place + jnp.where(low, 0, 2))
    second = take_lanes(second, place + jnp.where(low, 2, 0))
    return jnp.where(low, first, second), jnp.where(low, second, first)


def interleave(low_part, high_part, flip):
    lane = lane_index(low_part.shape)
    half = LANES // 2
    both = jnp.where(lane < half, low_part, high_part)
    is_odd = lane // 2 % 2
    upper = 1 - is_odd if flip else is_odd
    return take_lanes(both, lane // 4 * 2 + lane % 2 + upper * half)


def halves(x):
    high = x.astype(bf16)
    return high, (x - high.astype(f32)).astype(bf16)


def dot(a, b):
    return jnp.dot(a, b, preferred_element_type=f32)


def first_kernel(at_ref, *refs):
    *vel_refs, weight_ref, energy_ref, rest_ref, point_ref = refs
    step = pl.program_id(0)
    width = weight_ref.shape[1]
    weight = weight_ref[...]
    acc = None
    for lane in range(0, width, LANES):
        for vel_ref in vel_refs:
            x = vel_ref[0, :, lane : lane + LANES]
            term = x * x * weight[:, lane : lane + LANES]
            acc = term if acc is None else acc + term
    point_ref[...] = acc
    total = jnp.zeros((SUB, LANES), f32)
    high = jnp.zeros((SUB, LANES), f32)
    for n in range(NODES):
        part = point_ref[pl.ds(n, SUB, stride=NODES), :]
        total = total + part
        if IS_HIGH[n]:
            high = high + part

    @pl.when(step == 0)
    def _():
        energy_ref[...] = jnp.zeros(energy_ref.shape, f32)

    here = lane_index((SUB, LANES)) == step
    for q, part in enumerate((total, high)):
        energy_ref[q] = jnp.where(here, jnp.sum(part, axis=1, keepdims=True), energy_ref[q])

    @pl.when(step > 0)
    def _():
        rest_ref[pl.ds(pl.multiple_of((step - 1) * TILE, SUB), TILE), :] = vel_refs[-1][0]

    @pl.when(step == at_ref[0])
    def _():
        rest_ref[rest_ref.shape[0] - TILE :, :] = vel_refs[-2][0]


def first_pass(velocity, weight, there, lend):
    comps, points, width = velocity.shape
    shape = (2, SUB, LANES)
    rest = points if lend else points - TILE
    return pl.pallas_call(
        first_kernel,
        grid_spec=pltpu.PrefetchScalarGridSpec(
            num_scalar_prefetch=1,
            grid=(points // TILE,),
            in_specs=[
                *[pl.BlockSpec((1, TILE, width), lambda t, at, c=c: (c, t, 0)) for c in range(comps)],
                pl.BlockSpec((1, width), lambda t, at: (0, 0)),
            ],
            out_specs=[
                pl.BlockSpec(shape, lambda t, at: (0, 0, 0)),
                pl.BlockSpec((rest, width), lambda t, at: (0, 0)),
            ],
            scratch_shapes=[pltpu.VMEM((TILE, LANES), f32)],
        ),
        out_shape=[jax.ShapeDtypeStruct(shape, f32), jax.ShapeDtypeStruct((rest, width), f32)],
        compiler_params=pltpu.CompilerParams(vmem_limit_bytes=16 << 20),
        name="first_pass",
    )(there, *[velocity] * comps, weight)


def expand_kernel(inv_ref, spread_ref, out_ref):
    spread = spread_ref[...]
    for i in range(NODES):
        x = inv_ref[i]
        high, rest = halves(x)
        mid, low = halves(x - high.astype(f32))
        y = (dot(high, spread) + dot(mid, spread)) + dot(low, spread)
        for t in range(out_ref.shape[0]):
            out_ref[t, i] = y[:, t * LANES : (t + 1) * LANES]


def expand(inverses, width):
    pairs = inverses.shape[0]
    spread = np.repeat(np.eye(pairs), 2, axis=1).astype(ml_dtypes.bfloat16)
    return pl.pallas_call(
        expand_kernel,
        out_shape=jax.ShapeDtypeStruct((width // LANES, NODES, NODES, LANES), f32),
        compiler_params=pltpu.CompilerParams(vmem_limit_bytes=16 << 20),
        name="expand",
    )(jnp.transpose(inverses, (1, 2, 0)), spread)


def synthesis(blocks, synth_ref):
    tiles = [x[:, t : t + LANES] for x in blocks for t in range(0, x.shape[1], LANES)]
    pairs = [deinterleave(tiles[t], tiles[t + 1]) for t in range(0, len(tiles), 2)]
    sums = []
    for parity in (0, 1):
        high, low = halves(jnp.concatenate([p[parity] for p in pairs], axis=1))
        first = synth_ref[parity, 0]
        sums.append(dot(high, first) + dot(high, synth_ref[parity, 1]) + dot(low, first))
    return sums


def spanwise(near, away, width, derive_refs):
    parts = [halves(near + away), halves(near - away)]
    groups = []
    for derive_ref in derive_refs:
        span = []
        for parity, (high, low) in enumerate(parts):
            first = derive_ref[parity, 0]
            span.append(dot(high, first) + dot(high, derive_ref[parity, 1]) + dot(low, first))
        if width == LANES:
            groups.append([interleave(span[0], span[1], False)])
            continue
        tiles = []
        for t in range(width // LANES):
            at = slice(t // 2 * LANES, (t // 2 + 1) * LANES)
            tiles.append(interleave(span[t % 2][:, at], span[1 - t % 2][:, at], t % 2 == 1))
        groups.append(tiles)
    return groups


def element_solve(rhs_ref, res_ref, inv_ref):
    def solve(t, carry):
        right = [rhs_ref[t, pl.ds(n, SUB, stride=NODES), :] for n in range(NODES)]
        for i in range(NODES):
            acc = [None, None]
            for n in range(NODES):
                term = inv_ref[t, i, n : n + 1, :] * right[n]
                acc[n % 2] = term if n < 2 else acc[n % 2] + term
            res_ref[t, pl.ds(i, SUB, stride=NODES), :] = acc[0] + acc[1]
        return carry

    lax.fori_loop(0, inv_ref.shape[0], solve, 0)


def chunk_kernel(n_far, is_w, aliased, *refs):
    refs = list(refs)
    own_ref = refs.pop(0)
    far_refs = [refs.pop(0) for _ in range(n_far)]
    wphys_ref = None if is_w else refs.pop(0)
    damp_ref, synth_ref, derive_ref, inv_ref = refs[:4]
    refs = refs[4 + aliased :]
    out_ref = refs.pop(0)
    if is_w:
        wphys_ref = refs.pop(0)
    rhs_ref, res_ref = refs
    width = own_ref.shape[2]
    modes = wphys_ref.shape[1] // 2
    own = own_ref[0]
    even, odd = synthesis([own] + [r[...] for r in far_refs], synth_ref)
    near, away = even + odd, even - odd
    if is_w:
        wphys_ref[:, :modes] = near
        wphys_ref[:, modes:] = away
        near, away = near * near, away * away
    else:
        near, away = near * wphys_ref[:, :modes], away * wphys_ref[:, modes:]
    damp = damp_ref[...]
    for t, term in enumerate(spanwise(near, away, width, [derive_ref])[0]):
        x = own[:, t * LANES : (t + 1) * LANES]
        rhs_ref[t] = x - term - damp * x
    element_solve(rhs_ref, res_ref, inv_ref)
    for t in range(width // LANES):
        out_ref[0, :, t * LANES : (t + 1) * LANES] = res_ref[t]


def whole(shape):
    return pl.BlockSpec(shape, lambda *t: (0,) * len(shape), pipeline_mode=pl.Buffered(1))


def advance(velocity, far, comp, first, rows, wphys, damp, synth, derive, inv, out):
    comps, points, width = velocity.shape
    coefs = 2 * synth.shape[3]
    tiles = width // LANES
    is_w = comp == comps - 1
    at = first // TILE
    row = lambda w: pl.BlockSpec((TILE, w), lambda t: (at + t, 0))
    block = pl.BlockSpec((1, TILE, width), lambda t: (comp, at + t, 0))
    args = [velocity, *far]
    specs = [block] + [pl.BlockSpec((TILE, width), lambda t: (t, 0)) for _ in far]
    if not is_w:
        args.append(wphys)
        specs.append(row(coefs))
    args += [damp, synth, derive, inv]
    specs += [row(LANES), whole(synth.shape), whole(derive.shape), whole(inv.shape)]
    out_shape = [jax.ShapeDtypeStruct(velocity.shape, f32)]
    out_specs = [block]
    aliases = {}
    if out is not None:
        aliases[len(args)] = 0
        args.append(out)
        specs.append(pl.BlockSpec(memory_space=pl.ANY))
    if is_w:
        if wphys is not None:
            aliases[len(args)] = 1
            args.append(wphys)
            specs.append(pl.BlockSpec(memory_space=pl.ANY))
        out_shape.append(jax.ShapeDtypeStruct((points, coefs), f32))
        out_specs.append(row(coefs))
    result = pl.pallas_call(
        lambda *refs: chunk_kernel(len(far), is_w, len(aliases), *refs),
        grid=(rows // TILE,),
        in_specs=specs,
        out_specs=out_specs,
        out_shape=out_shape,
        scratch_shapes=[pltpu.VMEM((tiles, TILE, LANES), f32)] * 2,
        input_output_aliases=aliases,
        compiler_params=pltpu.CompilerParams(vmem_limit_bytes=14 << 20),
        cost_estimate=pl.CostEstimate(
            flops=3 * rows * coefs * (coefs + width), bytes_accessed=8 * rows * width, transcendentals=0
        ),
        name=f"advance_{comp}_{first}",
    )(*args)
    return (result[0], result[1] if is_w else wphys)


def both_kernel(at_ref, own_ref, far_ref, wphys_ref, synth_ref, derive_ref, other_ref, span_ref, *back_refs):
    modes = wphys_ref.shape[1] // 2
    width = far_ref.shape[1]
    even, odd = synthesis([own_ref[0], far_ref[...]], synth_ref)
    near = (even + odd) * wphys_ref[:, :modes]
    away = (even - odd) * wphys_ref[:, modes:]
    here, there = spanwise(near, away, width, [derive_ref, other_ref])
    for t, term in enumerate(here):
        span_ref[:, t * LANES : (t + 1) * LANES] = term
    for ref in back_refs:
        for t in range(0, ref.shape[1], LANES):
            ref[:, t : t + LANES] = there.pop(0)


def both_groups(velocity, comp, at, far, wphys, synth, derive, other, parts):
    width = velocity.shape[2]
    last = far.shape[0] // TILE - 1
    shapes = [(TILE, width)] + [(TILE, LANES * n) for n in parts]
    return pl.pallas_call(
        both_kernel,
        grid_spec=pltpu.PrefetchScalarGridSpec(
            num_scalar_prefetch=1,
            grid=(1,),
            in_specs=[
                pl.BlockSpec((1, TILE, width), lambda t, at: (comp, at[0], 0)),
                pl.BlockSpec((TILE, width), lambda t, at: (last, 0)),
                pl.BlockSpec((TILE, wphys.shape[1]), lambda t, at: (at[0], 0)),
                whole(synth.shape),
                whole(derive.shape),
                whole(other.shape),
            ],
            out_specs=[pl.BlockSpec(shape, lambda t, at: (0, 0)) for shape in shapes],
        ),
        out_shape=[jax.ShapeDtypeStruct(shape, f32) for shape in shapes],
        compiler_params=pltpu.CompilerParams(vmem_limit_bytes=14 << 20),
        name="both_groups",
    )(at, velocity, far, wphys, synth, derive, other)


def finish_kernel(at_ref, own_ref, span_ref, damp_ref, inv_ref, held_ref, out_ref):
    right = []
    for n in range(NODES):
        rows = pl.ds(n, SUB, stride=NODES)
        x = own_ref[0, rows, :]
        right.append(x - span_ref[rows, :] - damp_ref[rows, :] * x)
    for i in range(NODES):
        acc = [None, None]
        for n in range(NODES):
            term = inv_ref[0, i, n : n + 1, :] * right[n]
            acc[n % 2] = term if n < 2 else acc[n % 2] + term
        out_ref[0, pl.ds(i, SUB, stride=NODES), :] = acc[0] + acc[1]


def finish(velocity, comp, at, lane, span, damp, inv, out, name):
    block = pl.BlockSpec((1, TILE, LANES), lambda t, at: (comp, at[0], lane + t))
    return pl.pallas_call(
        finish_kernel,
        grid_spec=pltpu.PrefetchScalarGridSpec(
            num_scalar_prefetch=1,
            grid=(span.shape[1] // LANES,),
            in_specs=[
                block,
                pl.BlockSpec((TILE, LANES), lambda t, at: (0, t)),
                pl.BlockSpec((TILE, LANES), lambda t, at: (at[0], 0)),
                pl.BlockSpec((1, NODES, NODES, LANES), lambda t, at: (lane + t, 0, 0, 0)),
                pl.BlockSpec(memory_space=pl.ANY),
            ],
            out_specs=block,
        ),
        out_shape=jax.ShapeDtypeStruct(velocity.shape, f32),
        input_output_aliases={5: 0},
        compiler_params=pltpu.CompilerParams(vmem_limit_bytes=8 << 20),
        name=name,
    )(at, velocity, span, damp, inv, out)


def exchange(block):
    count = lax.axis_size("mode")
    return [
        lax.ppermute(block, "mode", [(i, (i + s) % count) for i in range(count)])
        for s in range(1, count)
    ]


def sum_over_plane(value):
    count = lax.axis_size("plane")
    if count & (count - 1):
        return lax.psum(value, "plane")
    step = 1
    while step < count:
        value = value + lax.ppermute(value, "plane", [(i, i ^ step) for i in range(count)])
        step *= 2
    return value


def on_device(velocity, inverses, neighbours, flags):
    mode_count = lax.axis_size("mode")
    plane_count = lax.axis_size("plane")
    mine = lax.axis_index("mode")
    comps, points, width = velocity.shape
    coefs = width * mode_count
    elements = neighbours.shape[0]
    w = comps - 1

    pieces = []
    for begin, end in ((0, HEAD), (HEAD, TILE)):
        first = velocity[w, begin:end]
        pieces.append(exchange(first))
        held, velocity = lax.optimization_barrier((first, velocity))
    far = {(w, 0, TILE): [jnp.concatenate(x) for x in zip(*pieces)]}
    index = mine * width + lax.iota(jnp.int32, width)
    weight = jnp.where(index < 2, 1.0, 2.0).astype(f32)[None, :]
    blocks = points // TILE
    shared = mode_count == 2 and width > LANES and blocks > 2
    here = jnp.reshape(blocks - 2 + mine, (1,))
    there = jnp.reshape(blocks - 1 - mine if shared else -1, (1,))
    packed, rest = first_pass(velocity, weight, there, shared)
    packed_far = exchange(packed)
    far[w, TILE, points - TILE] = exchange(rest)
    tail, velocity = lax.optimization_barrier((packed, velocity))
    for comp in range(w - 1):
        far[comp, 0, points] = exchange(velocity[comp])
    stop = points - 2 * TILE if shared else points
    for begin in range(0, stop, TILE):
        far[w - 1, begin, TILE] = exchange(velocity[w - 1, begin : begin + TILE])

    packed_far, far[w, 0, TILE] = lax.optimization_barrier((packed_far, far[w, 0, TILE]))
    steps = points // TILE
    parts = jnp.stack([x[:, :, :steps] for x in [packed] + packed_far])
    order = (mine - lax.iota(jnp.int32, mode_count)) % mode_count
    if mode_count == 2:
        sums = parts[0] + parts[1]
    else:
        sums = jnp.sum(jnp.take(parts, order, axis=0), axis=0)
    sums = jnp.transpose(sums, (0, 2, 1)).reshape(2, elements)
    total, high = sums[0], sums[1]
    field = sum_over_plane(jnp.sum(total))
    speed = jnp.sqrt(field / (1.0 * comps * points * plane_count * coefs))
    sensor = jnp.log10((high + 1e-06) / (total + 1e-06))
    ramp = 0.5 * (1.0 + jnp.sin(0.5 * math.pi * jnp.clip(sensor + 2.0, -1.0, 1.0)))
    shape = 0.4 * (1.0 + flags.astype(f32)) * ramp
    forward = [(i, i + 1) for i in range(plane_count - 1)]
    west = lax.ppermute(shape, "plane", forward)
    east = lax.ppermute(shape, "plane", [(b, a) for a, b in forward])
    source = speed * shape
    padded = speed * jnp.concatenate([west, shape, east])
    element = lax.iota(jnp.int32, elements)
    base = jnp.array([0, 2 * elements, elements, elements], dtype=jnp.int32)
    target = jnp.where(neighbours >= 0, base[None, :] + neighbours, elements + element[:, None])
    positions = lax.iota(jnp.int32, 3 * elements)
    picked = jnp.where(target[:, :, None] == positions[None, None, :], padded[None, None, :], 0.0)
    beside = jnp.sum(jnp.sum(picked, axis=2), axis=1)
    viscosity = (2.0 * source + beside) / 6.0
    node = np.arange(NODES)
    degrees = (node // (ORDER + 1)) ** 2 + (node % (ORDER + 1)) ** 2
    factor = (degrees / (2.0 * ORDER * ORDER)).astype(np.float32)
    damp = (viscosity[:, None] * factor[None, :]).reshape(points)
    damp = jnp.broadcast_to(damp[:, None], (points, LANES))

    synth_all, derive_all = (jnp.asarray(x) for x in tables(coefs, width))
    group = lambda table, at: lax.dynamic_index_in_dim(table, at, 0, keepdims=False)
    rows = [group(synth_all, order[s]) for s in range(mode_count)]
    swapped = rows if width > LANES else [rows[s ^ 1] for s in range(mode_count)]
    synth = jnp.stack([jnp.concatenate([x[p] for x in part], axis=1) for p, part in enumerate((rows, swapped))])
    derive = group(derive_all, mine)
    inv = expand(inverses, width)

    out = wphys = back = None
    for (comp, begin, count), blocks in far.items():
        if shared and back is None and comp != w:
            lent = far[w, TILE, points - TILE][0]
            other = group(derive_all, 1 - mine)
            parts = [width // LANES - 2, 1, 1] if width > 2 * LANES else [1, 1]
            span, *back = both_groups(velocity, w - 1, here, lent, wphys, synth, derive, other, parts)
            back = [exchange(x)[0] for x in back]
            out = finish(velocity, w - 1, here, 0, span, damp, inv, out, "finish_here")
        out, wphys = advance(velocity, blocks, comp, begin, count, wphys, damp, synth, derive, inv, out)
    if shared:
        lane = 0
        for term, count in zip(back, parts):
            out = finish(velocity, w - 1, there, lane, term, damp, inv, out, f"finish_there_{lane}")
            lane += count
    return (out, viscosity)


def solution(mesh):
    in_specs = (P(None, "plane", "mode"), P("mode", None, None), P("plane", None), P("plane"))
    out_specs = (P(None, "plane", "mode"), P("plane"))
    return jax.shard_map(
        on_device, mesh=mesh, in_specs=in_specs, out_specs=out_specs, check_vma=False
    )
```

```python
import math

import jax
import jax.numpy as jnp
import ml_dtypes
import numpy as np
from jax import lax
from jax.experimental import pallas as pl
from jax.experimental.pallas import tpu as pltpu
from jax.sharding import PartitionSpec as P

ORDER = 4
NODES = (ORDER + 1) ** 2
LENGTH = 4.0
LANES = 128
SUB = 8
TILE = SUB * NODES
HEAD = 64

f32 = jnp.float32
bf16 = jnp.bfloat16

IS_HIGH = [n // (ORDER + 1) == ORDER or n % (ORDER + 1) == ORDER for n in range(NODES)]


def split_np(table):
    high = table.astype(np.float32).astype(ml_dtypes.bfloat16)
    low = (table - high.astype(np.float64)).astype(ml_dtypes.bfloat16)
    return np.stack([high, low])


def parity_order(width):
    if width == LANES:
        index = np.arange(width)
        return index[index // 2 % 2 == 0], index[index // 2 % 2 == 1]
    index = np.arange(width).reshape(-1, 2, LANES)
    even = index[:, :, np.arange(LANES) // 2 % 2 == 0]
    odd = index[:, ::-1][:, :, np.arange(LANES) // 2 % 2 == 1]
    return even.reshape(-1), odd.reshape(-1)


def tables(coefs, width):
    modes = coefs // 2
    index = np.arange(coefs)
    pair = index // 2
    odd = index % 2
    freq = np.where(index == 1, modes, pair)
    angle = 2.0 * np.pi * (freq[:, None] * index[None, :modes] % coefs) / coefs
    use_cos = (odd == 0) | (pair == 0)
    basis = np.where(use_cos[:, None], np.cos(angle), -np.sin(angle))
    weight = np.where(pair == 0, 1.0, 2.0)
    rate = pair / (modes * LENGTH * math.sqrt(modes))
    partner = basis[index ^ 1]
    derive = (np.where(odd == 0, -rate, rate) / coefs)[:, None] * partner
    groups = coefs // width
    synth = (weight[:, None] * basis).reshape(groups, width, modes)
    derive = derive.reshape(groups, width, modes).transpose(0, 2, 1)
    orders = parity_order(width)
    synth = np.stack([split_np(synth[:, o]) for o in orders])
    derive = [derive[:, :, o] for o in orders]
    if width == LANES:
        derive = [np.pad(derive[p], ((0, 0), (0, 0), (p * LANES // 2, (1 - p) * LANES // 2))) for p in (0, 1)]
    derive = np.stack([split_np(d) for d in derive])
    return np.moveaxis(synth, 2, 0).copy(), np.moveaxis(derive, 2, 0).copy()


def lane_index(shape):
    return lax.broadcasted_iota(jnp.int32, shape, 1)


def take_lanes(x, index):
    return jnp.take_along_axis(x, index, axis=1, mode="promise_in_bounds")


def deinterleave(first, second):
    lane = lane_index(first.shape)
    half = LANES // 2
    low = lane < half
    place = 4 * (lane % half // 2) + lane % 2
    first = take_lanes(first, place + jnp.where(low, 0, 2))
    second = take_lanes(second, place + jnp.where(low, 2, 0))
    return jnp.where(low, first, second), jnp.where(low, second, first)


def interleave(low_part, high_part, flip):
    lane = lane_index(low_part.shape)
    half = LANES // 2
    both = jnp.where(lane < half, low_part, high_part)
    is_odd = lane // 2 % 2
    upper = 1 - is_odd if flip else is_odd
    return take_lanes(both, lane // 4 * 2 + lane % 2 + upper * half)


def halves(x):
    high = x.astype(bf16)
    return high, (x - high.astype(f32)).astype(bf16)


def dot(a, b):
    return jnp.dot(a, b, preferred_element_type=f32)


def first_kernel(at_ref, vel_ref, weight_ref, energy_ref, rest_ref, point_ref):
    step = pl.program_id(0)
    comps, _, width = vel_ref.shape
    weight = weight_ref[...]
    acc = None
    for lane in range(0, width, LANES):
        for comp in range(comps):
            x = vel_ref[comp, :, lane : lane + LANES]
            term = x * x * weight[:, lane : lane + LANES]
            acc = term if acc is None else acc + term
    point_ref[...] = acc
    total = jnp.zeros((SUB, LANES), f32)
    high = jnp.zeros((SUB, LANES), f32)
    for n in range(NODES):
        part = point_ref[pl.ds(n, SUB, stride=NODES), :]
        total = total + part
        if IS_HIGH[n]:
            high = high + part

    @pl.when(step == 0)
    def _():
        energy_ref[...] = jnp.zeros(energy_ref.shape, f32)

    here = lane_index((SUB, LANES)) == step
    for q, part in enumerate((total, high)):
        energy_ref[q] = jnp.where(here, jnp.sum(part, axis=1, keepdims=True), energy_ref[q])

    @pl.when(step > 0)
    def _():
        rest_ref[pl.ds(pl.multiple_of((step - 1) * TILE, SUB), TILE), :] = vel_ref[comps - 1]

    @pl.when(step == at_ref[0])
    def _():
        rest_ref[rest_ref.shape[0] - TILE :, :] = vel_ref[comps - 2]


def first_pass(velocity, weight, there, lend):
    comps, points, width = velocity.shape
    shape = (2, SUB, LANES)
    rest = points if lend else points - TILE
    return pl.pallas_call(
        first_kernel,
        grid_spec=pltpu.PrefetchScalarGridSpec(
            num_scalar_prefetch=1,
            grid=(points // TILE,),
            in_specs=[
                pl.BlockSpec((comps, TILE, width), lambda t, at: (0, t, 0)),
                pl.BlockSpec((1, width), lambda t, at: (0, 0)),
            ],
            out_specs=[
                pl.BlockSpec(shape, lambda t, at: (0, 0, 0)),
                pl.BlockSpec((rest, width), lambda t, at: (0, 0)),
            ],
            scratch_shapes=[pltpu.VMEM((TILE, LANES), f32)],
        ),
        out_shape=[jax.ShapeDtypeStruct(shape, f32), jax.ShapeDtypeStruct((rest, width), f32)],
        compiler_params=pltpu.CompilerParams(vmem_limit_bytes=16 << 20),
        name="first_pass",
    )(there, velocity, weight)


def expand_kernel(inv_ref, spread_ref, out_ref):
    spread = spread_ref[...]
    for i in range(NODES):
        x = inv_ref[i]
        high, rest = halves(x)
        mid, low = halves(x - high.astype(f32))
        y = (dot(high, spread) + dot(mid, spread)) + dot(low, spread)
        for t in range(out_ref.shape[0]):
            out_ref[t, i] = y[:, t * LANES : (t + 1) * LANES]


def expand(inverses, width):
    pairs = inverses.shape[0]
    spread = np.repeat(np.eye(pairs), 2, axis=1).astype(ml_dtypes.bfloat16)
    return pl.pallas_call(
        expand_kernel,
        out_shape=jax.ShapeDtypeStruct((width // LANES, NODES, NODES, LANES), f32),
        compiler_params=pltpu.CompilerParams(vmem_limit_bytes=16 << 20),
        name="expand",
    )(jnp.transpose(inverses, (1, 2, 0)), spread)


def synthesis(blocks, synth_ref):
    tiles = [x[:, t : t + LANES] for x in blocks for t in range(0, x.shape[1], LANES)]
    pairs = [deinterleave(tiles[t], tiles[t + 1]) for t in range(0, len(tiles), 2)]
    sums = []
    for parity in (0, 1):
        high, low = halves(jnp.concatenate([p[parity] for p in pairs], axis=1))
        first = synth_ref[parity, 0]
        sums.append(dot(high, first) + dot(high, synth_ref[parity, 1]) + dot(low, first))
    return sums


def spanwise(near, away, width, derive_refs):
    parts = [halves(near + away), halves(near - away)]
    groups = []
    for derive_ref in derive_refs:
        span = []
        for parity, (high, low) in enumerate(parts):
            first = derive_ref[parity, 0]
            span.append(dot(high, first) + dot(high, derive_ref[parity, 1]) + dot(low, first))
        if width == LANES:
            groups.append([interleave(span[0], span[1], False)])
            continue
        tiles = []
        for t in range(width // LANES):
            at = slice(t // 2 * LANES, (t // 2 + 1) * LANES)
            tiles.append(interleave(span[t % 2][:, at], span[1 - t % 2][:, at], t % 2 == 1))
        groups.append(tiles)
    return groups


def element_solve(rhs_ref, res_ref, inv_ref):
    def solve(t, carry):
        right = [rhs_ref[t, pl.ds(n, SUB, stride=NODES), :] for n in range(NODES)]
        for i in range(NODES):
            acc = [None, None]
            for n in range(NODES):
                term = inv_ref[t, i, n : n + 1, :] * right[n]
                acc[n % 2] = term if n < 2 else acc[n % 2] + term
            res_ref[t, pl.ds(i, SUB, stride=NODES), :] = acc[0] + acc[1]
        return carry

    lax.fori_loop(0, inv_ref.shape[0], solve, 0)


def chunk_kernel(n_far, is_w, aliased, *refs):
    refs = list(refs)
    own_ref = refs.pop(0)
    far_refs = [refs.pop(0) for _ in range(n_far)]
    wphys_ref = None if is_w else refs.pop(0)
    damp_ref, synth_ref, derive_ref, inv_ref = refs[:4]
    refs = refs[4 + aliased :]
    out_ref = refs.pop(0)
    if is_w:
        wphys_ref = refs.pop(0)
    rhs_ref, res_ref = refs
    width = own_ref.shape[2]
    modes = wphys_ref.shape[1] // 2
    own = own_ref[0]
    even, odd = synthesis([own] + [r[...] for r in far_refs], synth_ref)
    near, away = even + odd, even - odd
    if is_w:
        wphys_ref[:, :modes] = near
        wphys_ref[:, modes:] = away
        near, away = near * near, away * away
    else:
        near, away = near * wphys_ref[:, :modes], away * wphys_ref[:, modes:]
    damp = damp_ref[...]
    for t, term in enumerate(spanwise(near, away, width, [derive_ref])[0]):
        x = own[:, t * LANES : (t + 1) * LANES]
        rhs_ref[t] = x - term - damp * x
    element_solve(rhs_ref, res_ref, inv_ref)
    for t in range(width // LANES):
        out_ref[0, :, t * LANES : (t + 1) * LANES] = res_ref[t]


def whole(shape):
    return pl.BlockSpec(shape, lambda *t: (0,) * len(shape), pipeline_mode=pl.Buffered(1))


def advance(velocity, far, comp, first, rows, wphys, damp, synth, derive, inv, out):
    comps, points, width = velocity.shape
    coefs = 2 * synth.shape[3]
    tiles = width // LANES
    is_w = comp == comps - 1
    at = first // TILE
    row = lambda w: pl.BlockSpec((TILE, w), lambda t: (at + t, 0))
    block = pl.BlockSpec((1, TILE, width), lambda t: (comp, at + t, 0))
    args = [velocity, *far]
    specs = [block] + [pl.BlockSpec((TILE, width), lambda t: (t, 0)) for _ in far]
    if not is_w:
        args.append(wphys)
        specs.append(row(coefs))
    args += [damp, synth, derive, inv]
    specs += [row(LANES), whole(synth.shape), whole(derive.shape), whole(inv.shape)]
    out_shape = [jax.ShapeDtypeStruct(velocity.shape, f32)]
    out_specs = [block]
    aliases = {}
    if out is not None:
        aliases[len(args)] = 0
        args.append(out)
        specs.append(pl.BlockSpec(memory_space=pl.ANY))
    if is_w:
        if wphys is not None:
            aliases[len(args)] = 1
            args.append(wphys)
            specs.append(pl.BlockSpec(memory_space=pl.ANY))
        out_shape.append(jax.ShapeDtypeStruct((points, coefs), f32))
        out_specs.append(row(coefs))
    result = pl.pallas_call(
        lambda *refs: chunk_kernel(len(far), is_w, len(aliases), *refs),
        grid=(rows // TILE,),
        in_specs=specs,
        out_specs=out_specs,
        out_shape=out_shape,
        scratch_shapes=[pltpu.VMEM((tiles, TILE, LANES), f32)] * 2,
        input_output_aliases=aliases,
        compiler_params=pltpu.CompilerParams(vmem_limit_bytes=20 << 20),
        cost_estimate=pl.CostEstimate(
            flops=3 * rows * coefs * (coefs + width), bytes_accessed=8 * rows * width, transcendentals=0
        ),
        name=f"advance_{comp}_{first}",
    )(*args)
    return (result[0], result[1] if is_w else wphys)


def both_kernel(at_ref, own_ref, far_ref, wphys_ref, synth_ref, derive_ref, other_ref, span_ref, *back_refs):
    modes = wphys_ref.shape[1] // 2
    width = far_ref.shape[1]
    even, odd = synthesis([own_ref[0], far_ref[...]], synth_ref)
    near = (even + odd) * wphys_ref[:, :modes]
    away = (even - odd) * wphys_ref[:, modes:]
    here, there = spanwise(near, away, width, [derive_ref, other_ref])
    for t, term in enumerate(here):
        span_ref[:, t * LANES : (t + 1) * LANES] = term
    for ref in back_refs:
        for t in range(0, ref.shape[1], LANES):
            ref[:, t : t + LANES] = there.pop(0)


def both_groups(velocity, comp, at, far, wphys, synth, derive, other, parts):
    width = velocity.shape[2]
    last = far.shape[0] // TILE - 1
    shapes = [(TILE, width)] + [(TILE, LANES * n) for n in parts]
    return pl.pallas_call(
        both_kernel,
        grid_spec=pltpu.PrefetchScalarGridSpec(
            num_scalar_prefetch=1,
            grid=(1,),
            in_specs=[
                pl.BlockSpec((1, TILE, width), lambda t, at: (comp, at[0], 0)),
                pl.BlockSpec((TILE, width), lambda t, at: (last, 0)),
                pl.BlockSpec((TILE, wphys.shape[1]), lambda t, at: (at[0], 0)),
                whole(synth.shape),
                whole(derive.shape),
                whole(other.shape),
            ],
            out_specs=[pl.BlockSpec(shape, lambda t, at: (0, 0)) for shape in shapes],
        ),
        out_shape=[jax.ShapeDtypeStruct(shape, f32) for shape in shapes],
        compiler_params=pltpu.CompilerParams(vmem_limit_bytes=20 << 20),
        name="both_groups",
    )(at, velocity, far, wphys, synth, derive, other)


def finish_kernel(at_ref, own_ref, span_ref, damp_ref, inv_ref, held_ref, out_ref):
    right = []
    for n in range(NODES):
        rows = pl.ds(n, SUB, stride=NODES)
        x = own_ref[0, rows, :]
        right.append(x - span_ref[rows, :] - damp_ref[rows, :] * x)
    for i in range(NODES):
        acc = [None, None]
        for n in range(NODES):
            term = inv_ref[0, i, n : n + 1, :] * right[n]
            acc[n % 2] = term if n < 2 else acc[n % 2] + term
        out_ref[0, pl.ds(i, SUB, stride=NODES), :] = acc[0] + acc[1]


def finish(velocity, comp, at, lane, span, damp, inv, out, name):
    block = pl.BlockSpec((1, TILE, LANES), lambda t, at: (comp, at[0], lane + t))
    return pl.pallas_call(
        finish_kernel,
        grid_spec=pltpu.PrefetchScalarGridSpec(
            num_scalar_prefetch=1,
            grid=(span.shape[1] // LANES,),
            in_specs=[
                block,
                pl.BlockSpec((TILE, LANES), lambda t, at: (0, t)),
                pl.BlockSpec((TILE, LANES), lambda t, at: (at[0], 0)),
                pl.BlockSpec((1, NODES, NODES, LANES), lambda t, at: (lane + t, 0, 0, 0)),
                pl.BlockSpec(memory_space=pl.ANY),
            ],
            out_specs=block,
        ),
        out_shape=jax.ShapeDtypeStruct(velocity.shape, f32),
        input_output_aliases={5: 0},
        compiler_params=pltpu.CompilerParams(vmem_limit_bytes=8 << 20),
        name=name,
    )(at, velocity, span, damp, inv, out)


def exchange(block):
    count = lax.axis_size("mode")
    return [
        lax.ppermute(block, "mode", [(i, (i + s) % count) for i in range(count)])
        for s in range(1, count)
    ]


def sum_over_plane(value):
    count = lax.axis_size("plane")
    if count & (count - 1):
        return lax.psum(value, "plane")
    step = 1
    while step < count:
        value = value + lax.ppermute(value, "plane", [(i, i ^ step) for i in range(count)])
        step *= 2
    return value


def on_device(velocity, inverses, neighbours, flags):
    mode_count = lax.axis_size("mode")
    plane_count = lax.axis_size("plane")
    mine = lax.axis_index("mode")
    comps, points, width = velocity.shape
    coefs = width * mode_count
    elements = neighbours.shape[0]
    w = comps - 1

    pieces = []
    for begin, end in ((0, HEAD), (HEAD, TILE)):
        first = velocity[w, begin:end]
        pieces.append(exchange(first))
        held, velocity = lax.optimization_barrier((first, velocity))
    far = {(w, 0, TILE): [jnp.concatenate(x) for x in zip(*pieces)]}
    index = mine * width + lax.iota(jnp.int32, width)
    weight = jnp.where(index < 2, 1.0, 2.0).astype(f32)[None, :]
    blocks = points // TILE
    shared = mode_count == 2 and width > LANES and blocks > 2
    here = jnp.reshape(blocks - 2 + mine, (1,))
    there = jnp.reshape(blocks - 1 - mine if shared else -1, (1,))
    packed, rest = first_pass(velocity, weight, there, shared)
    packed_far = exchange(packed)
    far[w, TILE, points - TILE] = exchange(rest)
    tail, velocity = lax.optimization_barrier((packed, velocity))
    for comp in range(w - 1):
        far[comp, 0, points] = exchange(velocity[comp])
    stop = points - 2 * TILE if shared else points
    for begin in range(0, stop, TILE):
        far[w - 1, begin, TILE] = exchange(velocity[w - 1, begin : begin + TILE])

    packed_far, far[w, 0, TILE] = lax.optimization_barrier((packed_far, far[w, 0, TILE]))
    steps = points // TILE
    parts = jnp.stack([x[:, :, :steps] for x in [packed] + packed_far])
    order = (mine - lax.iota(jnp.int32, mode_count)) % mode_count
    if mode_count == 2:
        sums = parts[0] + parts[1]
    else:
        sums = jnp.sum(jnp.take(parts, order, axis=0), axis=0)
    sums = jnp.transpose(sums, (0, 2, 1)).reshape(2, elements)
    total, high = sums[0], sums[1]
    field = sum_over_plane(jnp.sum(total))
    speed = jnp.sqrt(field / (1.0 * comps * points * plane_count * coefs))
    sensor = jnp.log10((high + 1e-06) / (total + 1e-06))
    ramp = 0.5 * (1.0 + jnp.sin(0.5 * math.pi * jnp.clip(sensor + 2.0, -1.0, 1.0)))
    shape = 0.4 * (1.0 + flags.astype(f32)) * ramp
    forward = [(i, i + 1) for i in range(plane_count - 1)]
    west = lax.ppermute(shape, "plane", forward)
    east = lax.ppermute(shape, "plane", [(b, a) for a, b in forward])
    source = speed * shape
    padded = speed * jnp.concatenate([west, shape, east])
    element = lax.iota(jnp.int32, elements)
    base = jnp.array([0, 2 * elements, elements, elements], dtype=jnp.int32)
    target = jnp.where(neighbours >= 0, base[None, :] + neighbours, elements + element[:, None])
    positions = lax.iota(jnp.int32, 3 * elements)
    picked = jnp.where(target[:, :, None] == positions[None, None, :], padded[None, None, :], 0.0)
    beside = jnp.sum(jnp.sum(picked, axis=2), axis=1)
    viscosity = (2.0 * source + beside) / 6.0
    node = np.arange(NODES)
    degrees = (node // (ORDER + 1)) ** 2 + (node % (ORDER + 1)) ** 2
    factor = (degrees / (2.0 * ORDER * ORDER)).astype(np.float32)
    damp = (viscosity[:, None] * factor[None, :]).reshape(points)
    damp = jnp.broadcast_to(damp[:, None], (points, LANES))

    synth_all, derive_all = (jnp.asarray(x) for x in tables(coefs, width))
    group = lambda table, at: lax.dynamic_index_in_dim(table, at, 0, keepdims=False)
    rows = [group(synth_all, order[s]) for s in range(mode_count)]
    swapped = rows if width > LANES else [rows[s ^ 1] for s in range(mode_count)]
    synth = jnp.stack([jnp.concatenate([x[p] for x in part], axis=1) for p, part in enumerate((rows, swapped))])
    derive = group(derive_all, mine)
    inv = expand(inverses, width)

    out = wphys = back = None
    for (comp, begin, count), blocks in far.items():
        if shared and back is None and comp != w:
            lent = far[w, TILE, points - TILE][0]
            other = group(derive_all, 1 - mine)
            parts = [width // LANES - 2, 1, 1] if width > 2 * LANES else [1, 1]
            span, *back = both_groups(velocity, w - 1, here, lent, wphys, synth, derive, other, parts)
            back = [exchange(x)[0] for x in back]
            out = finish(velocity, w - 1, here, 0, span, damp, inv, out, "finish_here")
        out, wphys = advance(velocity, blocks, comp, begin, count, wphys, damp, synth, derive, inv, out)
    if shared:
        lane = 0
        for term, count in zip(back, parts):
            out = finish(velocity, w - 1, there, lane, term, damp, inv, out, f"finish_there_{lane}")
            lane += count
    return (out, viscosity)


def solution(mesh):
    in_specs = (P(None, "plane", "mode"), P("mode", None, None), P("plane", None), P("plane"))
    out_specs = (P(None, "plane", "mode"), P("plane"))
    return jax.shard_map(
        on_device, mesh=mesh, in_specs=in_specs, out_specs=out_specs, check_vma=False
    )
```
